768 devices in a mesh: replica: 4 (over x_lo, core), shard: 192 (over z, x_hi, y).
Axes of the slice: x: 4 (x_hi: 2, x_lo: 2; x = x_hi * 2 + x_lo), y: 8, z: 12, core: 2. Of those that a mesh axis runs over, the one named last changes fastest.
Arguments:
- activations: bfloat16 [4, 49152, 2, 192], P('replica', 'shard'), may hold values from -0.02734375 to 0.02734375
- out_grads: bfloat16 [4, 49152, 2, 4096], P('replica', 'shard'), may hold values from -6 to 6
- momentum: float32 [4, 192, 64, 128], P('replica', 'shard'), may hold values from -6 to 6
- band_idx: int32 [192, 2, 32], P('shard'), may hold values from 0 to 4095, as said below
Outputs:
- new_momentum: float32 [4, 192, 64, 128], P('replica', 'shard')
- update: float32 [192, 64, 128], P('shard')
The draws below stay inside these ranges and needn't reach their ends.
Inputs may be any that keep to these rules, and one draw needn't show every extreme that they name: `band_idx`: for each group and layer the 32 entries are distinct indices u * 64 + v of coefficients of the group's transform.
All inputs are finite; a program needn't handle non-finite values.
Results may differ from the reference program's by a relative error of at most 0.0003.
Values sent between devices are 32-bit elements; how exact they have to be, the bound alone decides.
No kernel may reach another device: no remote copies, remote signals or barrier semaphores. Data moves between devices by JAX's collectives and lax.ppermute only.
A program may use at most 64 MiB of HBM per device.

```python
import jax
import jax.numpy as jnp
from jax import lax

GROUP = 64
BAND = 32
LAYERS = 2
ROWBLOCKS = 3
COLS = 4096
TOKENS = 49152
ROWS = 192
GROUPS = 192
N_REPLICA = 4


def draw_band_idx(key, part):
    key = jax.random.fold_in(key, 7)
    row_keys = jax.random.split(key, GROUPS * LAYERS)

    def pick_row(row_key):
        return jax.random.permutation(row_key, GROUP * GROUP)[:BAND].astype(jnp.int32)
    picks = jax.vmap(pick_row)(row_keys)
    inner = jax.random.permutation(jax.random.fold_in(key, 11), GROUP * GROUP - 2)[:BAND - 2].astype(jnp.int32) + 1
    first_row = jnp.concatenate([jnp.array([0, GROUP * GROUP - 1], jnp.int32), inner])
    picks = picks.at[0].set(first_row)
    return picks.reshape(GROUPS, LAYERS, BAND).astype(jnp.int32)


def levels(rng, extent, cuts, smallest, largest):
    factor_of = 1.0
    for position, blocks in cuts:
        heights = jax.random.uniform(jax.random.fold_in(jax.random.fold_in(rng, 6), position), (blocks,), jnp.float32, smallest / len(cuts), largest / len(cuts))
        factor_of = factor_of * jnp.repeat(jnp.exp(heights), extent[position] // blocks).reshape((-1,) + (1,) * (len(extent) - 1 - position))
    return factor_of


def noise(own_key, dims, width, reach, shards=(), kind=jnp.bfloat16):
    level = levels(own_key, dims, shards, -0.22, 0.18) if shards else 1.0
    values = jax.random.normal(own_key, dims, jnp.float32) * width * level
    return jnp.minimum(jnp.maximum(values, -reach), reach).astype(kind)


def setup_inputs(seed: int = 0) -> dict:
    key_of = jax.random.split(jax.random.key(seed), 5)
    activations = noise(key_of[0], (N_REPLICA, TOKENS, LAYERS, ROWS), TOKENS ** -0.5, 0.02734375, ((0, 4), (1, 192)))
    out_grads = noise(key_of[1], (N_REPLICA, TOKENS, LAYERS, COLS), 1.0, 6.0, ((0, 4), (1, 192)))
    momentum = noise(key_of[2], (N_REPLICA, GROUPS, GROUP, LAYERS * GROUP), 1.0, 6.0, ((0, 4), (1, 192)), jnp.float32)
    band_idx = draw_band_idx(jax.random.fold_in(key_of[4], 71), 0)
    return {"activations": activations, "out_grads": out_grads, "momentum": momentum, "band_idx": band_idx}


MOMENTUM_DECAY = 0.999
DECODE_GAIN = 8.0

def dct_table(length):
    freq = jnp.arange(length, dtype=jnp.float32)[:, None]
    places = jnp.arange(length, dtype=jnp.float32)[None, :]
    scales = jnp.where(freq == 0, jnp.sqrt(1.0 / length), jnp.sqrt(2.0 / length)).astype(jnp.float32)
    return (scales * jnp.cos(jnp.pi * (2.0 * places + 1.0) * freq / (2.0 * length))).astype(jnp.float32)

def forward(tiles, matrix, layer_count):
    side = matrix.shape[0]
    left = jnp.einsum('ux,qxy->quy', matrix, tiles, precision=lax.Precision.HIGHEST)
    left = left.reshape(left.shape[0], side, layer_count, side)
    both = jnp.einsum('quly,vy->qulv', left, matrix, precision=lax.Precision.HIGHEST)
    return both.reshape(tiles.shape)

def inverse(coeffs, matrix, layer_count):
    side = matrix.shape[0]
    left = jnp.einsum('ux,quy->qxy', matrix, coeffs, precision=lax.Precision.HIGHEST)
    left = left.reshape(left.shape[0], side, layer_count, side)
    both = jnp.einsum('qxlv,vy->qxly', left, matrix, precision=lax.Precision.HIGHEST)
    return both.reshape(coeffs.shape)

def flat_positions(band_idx, side, layer_count):
    rows_u = band_idx // side
    cols_v = band_idx % side
    layer_ids = jnp.arange(layer_count, dtype=jnp.int32)[None, :, None]
    places = rows_u * (layer_count * side) + layer_ids * side + cols_v
    return places.reshape(band_idx.shape[0], -1).astype(jnp.int32)

def place_band(values, positions, total):
    group_ids = jnp.arange(positions.shape[0], dtype=jnp.int32)[:, None]
    empty = jnp.zeros((positions.shape[0], total), jnp.float32)
    return empty.at[group_ids, positions].set(values)

def replica_gradient(act_rows, grad_out):
    pieces = []
    for layer_idx in range(LAYERS):
        whole = jnp.dot(act_rows[:, layer_idx, :].T, grad_out[:, layer_idx, :], preferred_element_type=jnp.float32)
        whole = whole.reshape(ROWBLOCKS, GROUP, COLS // GROUP, GROUP).transpose(0, 2, 1, 3)
        pieces.append(whole.reshape(GROUPS, GROUP, GROUP))
    return jnp.concatenate(pieces, axis=2)

def reference(activations, out_grads, momentum, band_idx):
    matrix = dct_table(GROUP)
    positions = flat_positions(band_idx, GROUP, LAYERS)
    total = GROUP * LAYERS * GROUP
    gradient = lax.map(lambda item: replica_gradient(item[0], item[1]), (activations, out_grads))
    momentum_pre = MOMENTUM_DECAY * momentum + gradient
    new_list = []
    band_list = []
    for replica_id in range(N_REPLICA):
        coeffs = forward(momentum_pre[replica_id], matrix, LAYERS)
        band_vals = jnp.take_along_axis(coeffs.reshape(GROUPS, total), positions, axis=1)
        placed = place_band(band_vals, positions, total).reshape(coeffs.shape)
        new_list.append(momentum_pre[replica_id] - inverse(placed, matrix, LAYERS))
        band_list.append(band_vals)
    mean_band = lax.optimization_barrier(jnp.sum(jnp.stack(band_list), axis=0)) / N_REPLICA
    placed_mean = place_band(mean_band, positions, total).reshape(GROUPS, GROUP, LAYERS * GROUP)
    update = DECODE_GAIN * inverse(placed_mean, matrix, LAYERS)
    return (jnp.stack(new_list), update)
```

```python
import functools

import jax
import jax.numpy as jnp
import numpy as np
from jax import lax
from jax.experimental import pallas as pl
from jax.experimental.pallas import tpu as pltpu
from jax.sharding import PartitionSpec as P

MOMENTUM_DECAY = 0.999
DECODE_GAIN = 8.0
SIDE = 64
LAYERS = 2
WIDE = SIDE * LAYERS
BAND = 32
REPLICAS = 4
CHUNK = 512
HIGHEST = lax.Precision.HIGHEST


def flat(x_lo, core, z, x_hi, y):
    return ((x_lo * 2 + core) * 12 + z % 12) * 16 + x_hi * 8 + y % 8


def stage_groups():
    first, second, third = [], [], []
    for x_lo in range(2):
        for core in range(2):
            for x_hi in range(2):
                for z in range(core, 12 + core, 2):
                    for y in range(core, 8 + core, 2):
                        pz = sorted((z % 12, (z + 1) % 12), key=lambda v: v % 2)
                        py = sorted((y % 8, (y + 1) % 8), key=lambda v: v % 2)
                        first.append([flat(x_lo, core, a, x_hi, b) for a in pz for b in py])
            for z0 in range(2):
                for y0 in range(2):
                    for m in range(core, 6 + core, 2):
                        for n in range(core, 4 + core, 2):
                            pz = sorted((m % 6, (m + 1) % 6), key=lambda v: v % 2)
                            py = sorted((n % 4, (n + 1) % 4), key=lambda v: v % 2)
                            second.append(
                                [
                                    flat(x_lo, core, 2 * a + z0, h, 2 * b + y0)
                                    for h in range(2)
                                    for a in pz
                                    for b in py
                                ]
                            )
            for x_hi in range(2):
                for z in range(4):
                    for y in range(4):
                        third.append(
                            [flat(x_lo, core, 4 * a + z, x_hi, 4 * b + y) for a in range(3) for b in range(2)]
                        )
    return first, second, third


def dct_matrix():
    u = np.arange(SIDE, dtype=np.float64)[:, None]
    x = np.arange(SIDE, dtype=np.float64)[None, :]
    scale = np.where(u == 0, np.sqrt(1.0 / SIDE), np.sqrt(2.0 / SIDE))
    return (scale * np.cos(np.pi * (2.0 * x + 1.0) * u / (2.0 * SIDE))).astype(np.float32)


def terms_kernel(act_ref, grad_ref, out_ref, left_ref):
    tokens = grad_ref.shape[1]
    rows = act_ref.shape[1]

    @pl.when(pl.program_id(0) == 0)
    def _():
        token = lax.broadcasted_iota(jnp.int32, (tokens, tokens * LAYERS), 0)
        place = lax.broadcasted_iota(jnp.int32, (tokens, tokens * LAYERS), 1)
        for layer in range(LAYERS):
            spread = (place == token * LAYERS + layer).astype(jnp.float32).astype(act_ref.dtype)
            left_ref[layer * rows : (layer + 1) * rows] = jnp.dot(
                act_ref[layer], spread, preferred_element_type=jnp.float32
            ).astype(act_ref.dtype)

    rhs = grad_ref[0].reshape(tokens * LAYERS, CHUNK)
    both = jnp.dot(left_ref[...], rhs, preferred_element_type=jnp.float32)
    low = lax.broadcasted_iota(jnp.int32, (SIDE, WIDE), 1) < SIDE
    for a in range(rows // SIDE):
        for pair in range(CHUNK // WIDE):
            cols = slice(pair * WIDE, (pair + 1) * WIDE)
            one = both[a * SIDE : (a + 1) * SIDE, cols]
            two = both[rows + a * SIDE : rows + (a + 1) * SIDE, cols]
            even = jnp.where(low, one, pltpu.roll(two, SIDE, 1))
            odd = jnp.where(low, pltpu.roll(one, SIDE, 1), two)
            out_ref[0, 0, 0, 0, pair % 2, a, pair // 2] = even
            out_ref[0, 1, 0, 0, pair % 2, a, pair // 2] = odd


def gradient_terms(acts, grads):
    tokens, cols = grads.shape[1], grads.shape[3]
    rows = acts.shape[3]
    shape = (2, 2, 2, 2, 2, rows // SIDE, 2, SIDE, WIDE)
    return pl.pallas_call(
        terms_kernel,
        grid=(cols // CHUNK,),
        in_specs=[
            pl.BlockSpec((LAYERS, rows, tokens), lambda c: (0, 0, 0)),
            pl.BlockSpec((1, tokens, LAYERS, CHUNK), lambda c: (0, 0, 0, c)),
        ],
        out_specs=pl.BlockSpec(
            (1, 2, 1, 1, 2, rows // SIDE, 2, SIDE, WIDE),
            lambda c: ((c // 2) % 2, 0, c % 2, c // 4, 0, 0, 0, 0, 0),
        ),
        out_shape=jax.ShapeDtypeStruct(shape, jnp.float32),
        scratch_shapes=[pltpu.VMEM((LAYERS * rows, tokens * LAYERS), acts.dtype)],
        name="terms",
    )(acts[0].transpose(1, 2, 0), grads)


def dot(a, b, dims):
    return lax.dot_general(a, b, (dims, ((), ())), precision=HIGHEST, preferred_element_type=jnp.float32)


def one_hots(idx_ref):
    places = lax.broadcasted_iota(jnp.int32, (BAND, SIDE), 1)
    rows, cols = [], []
    for layer in range(LAYERS):
        idx = idx_ref[layer]
        rows.append((idx // SIDE == places).astype(jnp.float32))
        cols.append((idx % SIDE == places).astype(jnp.float32))
    masks = [dot(r, c, ((0,), (0,))) for r, c in zip(rows, cols)]
    return jnp.concatenate(masks, axis=1)


def encode_kernel(parts_ref, mom_ref, idx_ref, left_ref, wide_ref, new_ref, sent_ref):
    gradient = parts_ref[0]
    for k in range(1, parts_ref.shape[0]):
        gradient = gradient + parts_ref[k]
    pre = MOMENTUM_DECAY * mom_ref[0, 0] + gradient
    mask = one_hots(idx_ref)
    coeffs = dot(dot(left_ref[...], pre, ((1,), (0,))), wide_ref[...], ((1,), (1,)))
    kept = coeffs * mask
    for k in range(REPLICAS):
        sent_ref[k] = kept
    back = dot(dot(left_ref[...], kept, ((0,), (0,))), wide_ref[...], ((1,), (0,)))
    new_ref[0, 0] = pre - back


def decode_kernel(every_ref, left_ref, wide_ref, out_ref):
    mean = ((every_ref[0] + every_ref[1]) + (every_ref[2] + every_ref[3])) / REPLICAS
    back = dot(dot(left_ref[...], mean, ((0,), (0,))), wide_ref[...], ((1,), (0,)))
    out_ref[0] = DECODE_GAIN * back


def matrices():
    side = dct_matrix()
    return jnp.asarray(side), jnp.asarray(np.kron(np.eye(LAYERS, dtype=np.float32), side))


def encode(parts, momentum, band_idx):
    return pl.pallas_call(
        encode_kernel,
        out_shape=(
            jax.ShapeDtypeStruct((1, 1, SIDE, WIDE), jnp.float32),
            jax.ShapeDtypeStruct((REPLICAS, SIDE, WIDE), jnp.float32),
        ),
        name="encode",
    )(parts, momentum, band_idx.reshape(LAYERS, BAND, 1), *matrices())


def decode(every):
    return pl.pallas_call(
        decode_kernel,
        out_shape=jax.ShapeDtypeStruct((1, SIDE, WIDE), jnp.float32),
        name="decode",
    )(every, *matrices())


def local(acts, grads, momentum, band_idx):
    first, second, third = stage_groups()
    axes = ("replica", "shard")
    exchange = functools.partial(lax.all_to_all, axis_name=axes, split_axis=0, concat_axis=0, tiled=True)
    terms = gradient_terms(acts, grads).reshape(4, 48, SIDE, WIDE)
    terms = exchange(terms, axis_index_groups=first)
    terms = jnp.sum(terms, axis=0).reshape(8, 6, SIDE, WIDE)
    terms = exchange(terms, axis_index_groups=second)
    terms = jnp.sum(terms, axis=0)
    terms = exchange(terms, axis_index_groups=third)
    new_momentum, sent = encode(terms, momentum, band_idx)
    every = lax.all_to_all(sent, "replica", split_axis=0, concat_axis=0, tiled=True)
    update = decode(every)
    return (new_momentum, update)


def solution(mesh):
    return jax.shard_map(
        local,
        mesh=mesh,
        in_specs=(
            P("replica", "shard", None, None),
            P("replica", "shard", None, None),
            P("replica", "shard", None, None),
            P("shard", None, None),
        ),
        out_specs=(P("replica", "shard", None, None), P("shard", None, None)),
        check_vma=False,
    )
```

```python
import functools

import jax
import jax.numpy as jnp
import numpy as np
from jax import lax
from jax.experimental import pallas as pl
from jax.experimental.pallas import tpu as pltpu
from jax.sharding import PartitionSpec as P

MOMENTUM_DECAY = 0.999
DECODE_GAIN = 8.0
SIDE = 64
LAYERS = 2
WIDE = SIDE * LAYERS
BAND = 32
REPLICAS = 4
CHUNK = 512
HIGHEST = lax.Precision.HIGHEST


Z, Y = 12, 8


def flat(x_lo, core, z, x_hi, y):
    return ((x_lo * 2 + core) * Z + z % Z) * 16 + x_hi * 8 + y % Y


def partner(at, core, size):
    return (((at + size - core) ^ 1) + core) % size


def pairs(across_z, across_y):
    return [
        (
            flat(x_lo, core, z, x_hi, y),
            flat(
                x_lo,
                core,
                partner(z, core, Z) if across_z else z,
                x_hi,
                partner(y, core, Y) if across_y else y,
            ),
        )
        for x_lo in range(2)
        for core in range(2)
        for z in range(Z)
        for x_hi in range(2)
        for y in range(Y)
    ]


def stage_groups():
    second, third = [], []
    for x_lo in range(2):
        for core in range(2):
            for z0 in range(2):
                for y0 in range(2):
                    for m in range(core, 6 + core, 2):
                        for n in range(core, 4 + core, 2):
                            pz = sorted((m % 6, (m + 1) % 6), key=lambda v: v % 2)
                            py = sorted((n % 4, (n + 1) % 4), key=lambda v: v % 2)
                            second.append(
                                [
                                    flat(x_lo, core, 2 * a + z0, h, 2 * b + y0)
                                    for h in range(2)
                                    for a in pz
                                    for b in py
                                ]
                            )
            for x_hi in range(2):
                for z in range(4):
                    for y in range(4):
                        third.append(
                            [flat(x_lo, core, 4 * a + z, x_hi, 4 * b + y) for a in range(3) for b in range(2)]
                        )
    return second, third


def dct_matrix():
    u = np.arange(SIDE, dtype=np.float64)[:, None]
    x = np.arange(SIDE, dtype=np.float64)[None, :]
    scale = np.where(u == 0, np.sqrt(1.0 / SIDE), np.sqrt(2.0 / SIDE))
    return (scale * np.cos(np.pi * (2.0 * x + 1.0) * u / (2.0 * SIDE))).astype(np.float32)


def parities(place_ref):
    return (place_ref[0] >> 4) & 1, place_ref[0] & 1


def terms_kernel(place_ref, act_ref, grad_ref, other_ref, own_ref, left_ref):
    tokens = grad_ref.shape[1]
    rows = act_ref.shape[1]

    @pl.when(pl.program_id(0) == 0)
    def _():
        token = lax.broadcasted_iota(jnp.int32, (tokens, tokens * LAYERS), 0)
        place = lax.broadcasted_iota(jnp.int32, (tokens, tokens * LAYERS), 1)
        for layer in range(LAYERS):
            spread = (place == token * LAYERS + layer).astype(jnp.float32).astype(act_ref.dtype)
            left_ref[layer * rows : (layer + 1) * rows] = jnp.dot(
                act_ref[layer], spread, preferred_element_type=jnp.float32
            ).astype(act_ref.dtype)

    rhs = grad_ref[0].reshape(tokens * LAYERS, CHUNK)
    both = jnp.dot(left_ref[...], rhs, preferred_element_type=jnp.float32)
    low = lax.broadcasted_iota(jnp.int32, (SIDE, WIDE), 1) < SIDE

    def write(even_ref, odd_ref):
        for a in range(rows // SIDE):
            for pair in range(CHUNK // WIDE):
                cols = slice(pair * WIDE, (pair + 1) * WIDE)
                one = both[a * SIDE : (a + 1) * SIDE, cols]
                two = both[rows + a * SIDE : rows + (a + 1) * SIDE, cols]
                even_ref[0, 0, pair % 2, a, pair // 2] = jnp.where(low, one, pltpu.roll(two, SIDE, 1))
                odd_ref[0, 0, pair % 2, a, pair // 2] = jnp.where(low, pltpu.roll(one, SIDE, 1), two)

    @pl.when(parities(place_ref)[1] == 0)
    def _():
        write(own_ref, other_ref)

    @pl.when(parities(place_ref)[1] == 1)
    def _():
        write(other_ref, own_ref)


def gradient_terms(place, acts, grads, far):
    tokens, cols = grads.shape[1], grads.shape[3]
    rows = acts.shape[1]
    out = jax.ShapeDtypeStruct((2, 2, 2, rows // SIDE, 2, SIDE, WIDE), jnp.float32)
    out_spec = pl.BlockSpec(
        (1, 1, 2, rows // SIDE, 2, SIDE, WIDE), lambda c, place: (c % 2, c // 2, 0, 0, 0, 0, 0)
    )
    return pl.pallas_call(
        terms_kernel,
        grid_spec=pltpu.PrefetchScalarGridSpec(
            num_scalar_prefetch=1,
            grid=(cols // CHUNK // 2,),
            in_specs=[
                pl.BlockSpec((LAYERS, rows, tokens), lambda c, place: (0, 0, 0)),
                pl.BlockSpec(
                    (1, tokens, LAYERS, CHUNK),
                    lambda c, place: (0, 0, 0, (c // 2) * 4 + (parities(place)[0] ^ far) * 2 + c % 2),
                ),
            ],
            out_specs=[out_spec, out_spec],
            scratch_shapes=[pltpu.VMEM((LAYERS * rows, tokens * LAYERS), acts.dtype)],
        ),
        out_shape=(out, out),
        compiler_params=pltpu.CompilerParams(vmem_limit_bytes=16 * 2**20),
        name="far" if far else "near",
    )(place, acts, grads)


def dot(a, b, dims):
    return lax.dot_general(a, b, (dims, ((), ())), precision=HIGHEST, preferred_element_type=jnp.float32)


def one_hots(idx_ref):
    places = lax.broadcasted_iota(jnp.int32, (BAND, SIDE), 1)
    rows, cols = [], []
    for layer in range(LAYERS):
        idx = idx_ref[layer]
        rows.append((idx // SIDE == places).astype(jnp.float32))
        cols.append((idx % SIDE == places).astype(jnp.float32))
    masks = [dot(r, c, ((0,), (0,))) for r, c in zip(rows, cols)]
    return jnp.concatenate(masks, axis=1)


def encode_kernel(parts_ref, mom_ref, idx_ref, left_ref, wide_ref, new_ref, sent_ref):
    gradient = parts_ref[0]
    for k in range(1, parts_ref.shape[0]):
        gradient = gradient + parts_ref[k]
    pre = MOMENTUM_DECAY * mom_ref[0, 0] + gradient
    mask = one_hots(idx_ref)
    coeffs = dot(dot(left_ref[...], pre, ((1,), (0,))), wide_ref[...], ((1,), (1,)))
    kept = coeffs * mask
    for k in range(REPLICAS):
        sent_ref[k] = kept
    back = dot(dot(left_ref[...], kept, ((0,), (0,))), wide_ref[...], ((1,), (0,)))
    new_ref[0, 0] = pre - back


def decode_kernel(every_ref, left_ref, wide_ref, out_ref):
    mean = ((every_ref[0] + every_ref[1]) + (every_ref[2] + every_ref[3])) / REPLICAS
    back = dot(dot(left_ref[...], mean, ((0,), (0,))), wide_ref[...], ((1,), (0,)))
    out_ref[0] = DECODE_GAIN * back


def matrices():
    side = dct_matrix()
    return jnp.asarray(side), jnp.asarray(np.kron(np.eye(LAYERS, dtype=np.float32), side))


def encode(parts, momentum, band_idx):
    return pl.pallas_call(
        encode_kernel,
        out_shape=(
            jax.ShapeDtypeStruct((1, 1, SIDE, WIDE), jnp.float32),
            jax.ShapeDtypeStruct((REPLICAS, SIDE, WIDE), jnp.float32),
        ),
        compiler_params=pltpu.CompilerParams(vmem_limit_bytes=4 * 2**20),
        name="encode",
    )(parts, momentum, band_idx.reshape(LAYERS, BAND, 1), *matrices())


def decode(every):
    return pl.pallas_call(
        decode_kernel,
        out_shape=jax.ShapeDtypeStruct((1, SIDE, WIDE), jnp.float32),
        compiler_params=pltpu.CompilerParams(vmem_limit_bytes=4 * 2**20),
        name="decode",
    )(every, *matrices())


def local(acts, grads, momentum, band_idx):
    second, third = stage_groups()
    axes = ("replica", "shard")
    exchange = functools.partial(lax.all_to_all, axis_name=axes, split_axis=0, concat_axis=0, tiled=True)
    place = lax.axis_index(axes)[None]
    acts = acts[0].transpose(1, 2, 0)
    diagonal, across_z = gradient_terms(place, acts, grads, 1)
    across_y, own = gradient_terms(place, acts, grads, 0)
    diagonal = lax.ppermute(diagonal, axes, pairs(True, True))
    across_z = lax.ppermute(across_z, axes, pairs(True, False))
    across_y = lax.ppermute(across_y, axes, pairs(False, True))
    terms = ((own + across_y) + (across_z + diagonal)).reshape(8, 6, SIDE, WIDE)
    terms = exchange(terms, axis_index_groups=second)
    terms = jnp.sum(terms, axis=0)
    terms = exchange(terms, axis_index_groups=third)
    new_momentum, sent = encode(terms, momentum, band_idx)
    every = lax.all_to_all(sent, "replica", split_axis=0, concat_axis=0, tiled=True)
    update = decode(every)
    return (new_momentum, update)


def solution(mesh):
    return jax.shard_map(
        local,
        mesh=mesh,
        in_specs=(
            P("replica", "shard", None, None),
            P("replica", "shard", None, None),
            P("replica", "shard", None, None),
            P("shard", None, None),
        ),
        out_specs=(P("replica", "shard", None, None), P("shard", None, None)),
        check_vma=False,
    )
```

```python
import functools

import jax
import jax.numpy as jnp
import numpy as np
from jax import lax
from jax.experimental import pallas as pl
from jax.experimental.pallas import tpu as pltpu
from jax.sharding import PartitionSpec as P

MOMENTUM_DECAY = 0.999
DECODE_GAIN = 8.0
SIDE = 64
LAYERS = 2
WIDE = SIDE * LAYERS
BAND = 32
REPLICAS = 4
CHUNK = 512
HIGHEST = lax.Precision.HIGHEST


Z, Y = 12, 8


def flat(x_lo, core, z, x_hi, y):
    return ((x_lo * 2 + core) * Z + z % Z) * 16 + x_hi * 8 + y % Y


def partner(at, core, size):
    return (((at + size - core) ^ 1) + core) % size


def pairs(across_z, across_y):
    return [
        (
            flat(x_lo, core, z, x_hi, y),
            flat(
                x_lo,
                core,
                partner(z, core, Z) if across_z else z,
                x_hi,
                partner(y, core, Y) if across_y else y,
            ),
        )
        for x_lo in range(2)
        for core in range(2)
        for z in range(Z)
        for x_hi in range(2)
        for y in range(Y)
    ]


def stage_groups():
    second, third = [], []
    for x_lo in range(2):
        for core in range(2):
            for z0 in range(2):
                for y0 in range(2):
                    for m in range(core, 6 + core, 2):
                        for n in range(core, 4 + core, 2):
                            pz = sorted((m % 6, (m + 1) % 6), key=lambda v: v % 2)
                            py = sorted((n % 4, (n + 1) % 4), key=lambda v: v % 2)
                            second.append(
                                [
                                    flat(x_lo, core, 2 * a + z0, h, 2 * b + y0)
                                    for h in range(2)
                                    for a in pz
                                    for b in py
                                ]
                            )
            for x_hi in range(2):
                for z in range(4):
                    for y in range(4):
                        third.append(
                            [flat(x_lo, core, 4 * a + z, x_hi, 4 * b + y) for a in range(3) for b in range(2)]
                        )
    return second, third


def dct_matrix():
    u = np.arange(SIDE, dtype=np.float64)[:, None]
    x = np.arange(SIDE, dtype=np.float64)[None, :]
    scale = np.where(u == 0, np.sqrt(1.0 / SIDE), np.sqrt(2.0 / SIDE))
    return (scale * np.cos(np.pi * (2.0 * x + 1.0) * u / (2.0 * SIDE))).astype(np.float32)


def parities(place_ref):
    return (place_ref[0] >> 4) & 1, place_ref[0] & 1


def terms_kernel(colour, place_ref, act_ref, grad_ref, send_ref, keep_ref, left_ref):
    tokens = grad_ref.shape[1]
    rows = act_ref.shape[1]
    _, y_own = parities(place_ref)

    @pl.when((pl.program_id(0) == 0) & (pl.program_id(1) == 0))
    def _():
        token = lax.broadcasted_iota(jnp.int32, (tokens, tokens * LAYERS), 0)
        place = lax.broadcasted_iota(jnp.int32, (tokens, tokens * LAYERS), 1)
        for layer in range(LAYERS):
            spread = (place == token * LAYERS + layer).astype(jnp.float32).astype(act_ref.dtype)
            left_ref[layer * rows : (layer + 1) * rows] = jnp.dot(
                act_ref[layer], spread, preferred_element_type=jnp.float32
            ).astype(act_ref.dtype)

    rhs = grad_ref[0].reshape(tokens * LAYERS, CHUNK)
    both = jnp.dot(left_ref[...], rhs, preferred_element_type=jnp.float32)
    low = lax.broadcasted_iota(jnp.int32, (SIDE, WIDE), 1) < SIDE

    def write(even_ref, odd_ref, even_at, odd_at):
        for a in range(rows // SIDE):
            for pair in range(CHUNK // WIDE):
                cols = slice(pair * WIDE, (pair + 1) * WIDE)
                one = both[a * SIDE : (a + 1) * SIDE, cols]
                two = both[rows + a * SIDE : rows + (a + 1) * SIDE, cols]
                even_ref[even_at, 0, pair % 2, a, pair // 2] = jnp.where(low, one, pltpu.roll(two, SIDE, 1))
                odd_ref[odd_at, 0, pair % 2, a, pair // 2] = jnp.where(low, pltpu.roll(one, SIDE, 1), two)

    if colour == 0:
        pl.when(y_own == 0)(lambda: write(keep_ref, send_ref, 0, 0))
        pl.when(y_own == 1)(lambda: write(send_ref, keep_ref, 0, 0))
    else:
        pl.when(pl.program_id(0) == 0)(lambda: write(send_ref, send_ref, 1 - y_own, y_own))
        pl.when(pl.program_id(0) == 1)(lambda: write(keep_ref, keep_ref, 1 - y_own, y_own))


def gradient_terms(place, acts, grads, colour):
    tokens = grads.shape[1]
    rows = acts.shape[1]
    out = jax.ShapeDtypeStruct((2, 2, 2, rows // SIDE, 2, SIDE, WIDE), jnp.float32)
    block = (2 if colour else 1, 1, 2, rows // SIDE, 2, SIDE, WIDE)
    if colour == 0:
        send_spec = keep_spec = pl.BlockSpec(block, lambda z, k, place: (z, k, 0, 0, 0, 0, 0))
    else:
        send_spec = pl.BlockSpec(block, lambda z, k, place: (0, jnp.where(z == 0, k, 1), 0, 0, 0, 0, 0))
        keep_spec = pl.BlockSpec(block, lambda z, k, place: (0, jnp.where(z == 0, 0, k), 0, 0, 0, 0, 0))
    return pl.pallas_call(
        functools.partial(terms_kernel, colour),
        grid_spec=pltpu.PrefetchScalarGridSpec(
            num_scalar_prefetch=1,
            grid=(2, 2),
            in_specs=[
                pl.BlockSpec((LAYERS, rows, tokens), lambda z, k, place: (0, 0, 0)),
                pl.BlockSpec(
                    (1, tokens, LAYERS, CHUNK),
                    lambda z, k, place: (0, 0, 0, k * 4 + (parities(place)[0] ^ 1 ^ z) * 2 + colour),
                ),
            ],
            out_specs=[send_spec, keep_spec],
            scratch_shapes=[pltpu.VMEM((LAYERS * rows, tokens * LAYERS), acts.dtype)],
        ),
        out_shape=(out, out),
        compiler_params=pltpu.CompilerParams(vmem_limit_bytes=16 * 2**20),
        name=f"terms{colour}",
    )(place, acts, grads)


def dot(a, b, dims):
    return lax.dot_general(a, b, (dims, ((), ())), precision=HIGHEST, preferred_element_type=jnp.float32)


def one_hots(idx_ref):
    places = lax.broadcasted_iota(jnp.int32, (BAND, SIDE), 1)
    rows, cols = [], []
    for layer in range(LAYERS):
        idx = idx_ref[layer]
        rows.append((idx // SIDE == places).astype(jnp.float32))
        cols.append((idx % SIDE == places).astype(jnp.float32))
    masks = [dot(r, c, ((0,), (0,))) for r, c in zip(rows, cols)]
    return jnp.concatenate(masks, axis=1)


def encode_kernel(parts_ref, mom_ref, idx_ref, left_ref, wide_ref, new_ref, sent_ref):
    gradient = parts_ref[0]
    for k in range(1, parts_ref.shape[0]):
        gradient = gradient + parts_ref[k]
    pre = MOMENTUM_DECAY * mom_ref[0, 0] + gradient
    mask = one_hots(idx_ref)
    coeffs = dot(dot(left_ref[...], pre, ((1,), (0,))), wide_ref[...], ((1,), (1,)))
    kept = coeffs * mask
    for k in range(REPLICAS):
        sent_ref[k] = kept
    back = dot(dot(left_ref[...], kept, ((0,), (0,))), wide_ref[...], ((1,), (0,)))
    new_ref[0, 0] = pre - back


def decode_kernel(every_ref, left_ref, wide_ref, out_ref):
    mean = ((every_ref[0] + every_ref[1]) + (every_ref[2] + every_ref[3])) / REPLICAS
    back = dot(dot(left_ref[...], mean, ((0,), (0,))), wide_ref[...], ((1,), (0,)))
    out_ref[0] = DECODE_GAIN * back


def matrices():
    side = dct_matrix()
    return jnp.asarray(side), jnp.asarray(np.kron(np.eye(LAYERS, dtype=np.float32), side))


def encode(parts, momentum, band_idx):
    return pl.pallas_call(
        encode_kernel,
        out_shape=(
            jax.ShapeDtypeStruct((1, 1, SIDE, WIDE), jnp.float32),
            jax.ShapeDtypeStruct((REPLICAS, SIDE, WIDE), jnp.float32),
        ),
        compiler_params=pltpu.CompilerParams(vmem_limit_bytes=4 * 2**20),
        name="encode",
    )(parts, momentum, band_idx.reshape(LAYERS, BAND, 1), *matrices())


def decode(every):
    return pl.pallas_call(
        decode_kernel,
        out_shape=jax.ShapeDtypeStruct((1, SIDE, WIDE), jnp.float32),
        compiler_params=pltpu.CompilerParams(vmem_limit_bytes=4 * 2**20),
        name="decode",
    )(every, *matrices())


def local(acts, grads, momentum, band_idx):
    second, third = stage_groups()
    axes = ("replica", "shard")
    exchange = functools.partial(lax.all_to_all, axis_name=axes, split_axis=0, concat_axis=0, tiled=True)
    place = lax.axis_index(axes)[None]
    acts = acts[0].transpose(1, 2, 0)
    hop = functools.partial(lax.ppermute, axis_name=axes)
    across_z, across_y = pairs(True, False), pairs(False, True)
    ways = [(across_y, across_z), (across_z, across_y)]
    sums = []
    for colour in range(2):
        send, keep = gradient_terms(place, acts, grads, colour)
        got = hop(send, perm=ways[colour][0])
        got, more = keep[1] + got[1], hop(keep[0] + got[0], perm=ways[colour][1])
        sums.append(got + more)
    terms = jnp.concatenate(sums).reshape(8, 6, SIDE, WIDE)
    terms = exchange(terms, axis_index_groups=second)
    terms = jnp.sum(terms, axis=0)
    terms = exchange(terms, axis_index_groups=third)
    new_momentum, sent = encode(terms, momentum, band_idx)
    every = lax.all_to_all(sent, "replica", split_axis=0, concat_axis=0, tiled=True)
    update = decode(every)
    return (new_momentum, update)


def solution(mesh):
    return jax.shard_map(
        local,
        mesh=mesh,
        in_specs=(
            P("replica", "shard", None, None),
            P("replica", "shard", None, None),
            P("replica", "shard", None, None),
            P("shard", None, None),
        ),
        out_specs=(P("replica", "shard", None, None), P("shard", None, None)),
        check_vma=False,
    )
```

```python
import functools

import jax
import jax.numpy as jnp
import numpy as np
from jax import lax
from jax.experimental import pallas as pl
from jax.experimental.pallas import tpu as pltpu
from jax.sharding import PartitionSpec as P

MOMENTUM_DECAY = 0.999
DECODE_GAIN = 8.0
SIDE = 64
LAYERS = 2
WIDE = SIDE * LAYERS
BAND = 32
REPLICAS = 4
CHUNK = 512
FIRST_VMEM = 50
HIGHEST = lax.Precision.HIGHEST


Z, Y = 12, 8


def flat(x_lo, core, z, x_hi, y):
    return ((x_lo * 2 + core) * Z + z % Z) * 16 + x_hi * 8 + y % Y


def partner(at, core, size):
    return (((at + size - core) ^ 1) + core) % size


def pairs(across_z, across_y):
    return [
        (
            flat(x_lo, core, z, x_hi, y),
            flat(
                x_lo,
                core,
                partner(z, core, Z) if across_z else z,
                x_hi,
                partner(y, core, Y) if across_y else y,
            ),
        )
        for x_lo in range(2)
        for core in range(2)
        for z in range(Z)
        for x_hi in range(2)
        for y in range(Y)
    ]


def stage_groups():
    second, third = [], []
    for x_lo in range(2):
        for core in range(2):
            for z0 in range(2):
                for y0 in range(2):
                    for m in range(core, 6 + core, 2):
                        for n in range(core, 4 + core, 2):
                            pz = sorted((m % 6, (m + 1) % 6), key=lambda v: v % 2)
                            py = sorted((n % 4, (n + 1) % 4), key=lambda v: v % 2)
                            second.append(
                                [
                                    flat(x_lo, core, 2 * a + z0, h, 2 * b + y0)
                                    for h in range(2)
                                    for a in pz
                                    for b in py
                                ]
                            )
            for x_hi in range(2):
                for z in range(4):
                    for y in range(4):
                        third.append(
                            [flat(x_lo, core, 4 * a + z, x_hi, 4 * b + y) for a in range(3) for b in range(2)]
                        )
    return second, third


def dct_matrix():
    u = np.arange(SIDE, dtype=np.float64)[:, None]
    x = np.arange(SIDE, dtype=np.float64)[None, :]
    scale = np.where(u == 0, np.sqrt(1.0 / SIDE), np.sqrt(2.0 / SIDE))
    return (scale * np.cos(np.pi * (2.0 * x + 1.0) * u / (2.0 * SIDE))).astype(np.float32)


def parities(place_ref):
    return (place_ref[0] >> 4) & 1, place_ref[0] & 1


def left_kernel_part(act_ref, left_ref):
    rows, tokens = act_ref.shape[1:]
    token = lax.broadcasted_iota(jnp.int32, (tokens, tokens * LAYERS), 0)
    place = lax.broadcasted_iota(jnp.int32, (tokens, tokens * LAYERS), 1)
    for layer in range(LAYERS):
        spread = (place == token * LAYERS + layer).astype(jnp.float32).astype(act_ref.dtype)
        left_ref[layer * rows : (layer + 1) * rows] = jnp.dot(
            act_ref[layer], spread, preferred_element_type=jnp.float32
        ).astype(act_ref.dtype)


def terms_kernel(first, place_ref, in_ref, grad_ref, other_ref, own_ref, *made_ref):
    tokens = grad_ref.shape[1]
    if first:
        left_ref = made_ref[0]
        pl.when(pl.program_id(0) == 0)(lambda: left_kernel_part(in_ref, left_ref))
    else:
        left_ref = in_ref
    rows = left_ref.shape[0] // LAYERS
    rhs = grad_ref[0].reshape(tokens * LAYERS, CHUNK)
    both = jnp.dot(left_ref[...], rhs, preferred_element_type=jnp.float32)
    low = lax.broadcasted_iota(jnp.int32, (SIDE, WIDE), 1) < SIDE

    def write(even_ref, odd_ref):
        for a in range(rows // SIDE):
            for pair in range(CHUNK // WIDE):
                cols = slice(pair * WIDE, (pair + 1) * WIDE)
                one = both[a * SIDE : (a + 1) * SIDE, cols]
                two = both[rows + a * SIDE : rows + (a + 1) * SIDE, cols]
                even_ref[0, pair % 2, a, pair // 2] = jnp.where(low, one, pltpu.roll(two, SIDE, 1))
                odd_ref[0, pair % 2, a, pair // 2] = jnp.where(low, pltpu.roll(one, SIDE, 1), two)

    _, y_own = parities(place_ref)
    pl.when(y_own == 0)(lambda: write(own_ref, other_ref))
    pl.when(y_own == 1)(lambda: write(other_ref, own_ref))


def gradient_terms(place, acts_or_left, grads, colour, far):
    first = acts_or_left.ndim == 3
    tokens = grads.shape[1]
    rows = acts_or_left.shape[1] if first else acts_or_left.shape[0] // LAYERS
    blocks = (2, 2, rows // SIDE, 2, SIDE, WIDE)
    out = jax.ShapeDtypeStruct(blocks, jnp.float32)
    out_spec = pl.BlockSpec((1,) + blocks[1:], lambda k, place: (k, 0, 0, 0, 0, 0))
    left = (LAYERS * rows, tokens * LAYERS)
    left_spec = pl.BlockSpec(left, lambda k, place: (0, 0))
    return pl.pallas_call(
        functools.partial(terms_kernel, first),
        grid_spec=pltpu.PrefetchScalarGridSpec(
            num_scalar_prefetch=1,
            grid=(2,),
            in_specs=[
                pl.BlockSpec(acts_or_left.shape, lambda k, place: (0, 0, 0)) if first else left_spec,
                pl.BlockSpec(
                    (1, tokens, LAYERS, CHUNK),
                    lambda k, place: (0, 0, 0, k * 4 + (parities(place)[0] ^ far) * 2 + colour),
                ),
            ],
            out_specs=[out_spec, out_spec] + [left_spec] * first,
        ),
        out_shape=[out, out] + [jax.ShapeDtypeStruct(left, acts_or_left.dtype)] * first,
        compiler_params=pltpu.CompilerParams(vmem_limit_bytes=(FIRST_VMEM if first else 40) * 2**20),
        name=f"terms{colour}{far}",
    )(place, acts_or_left, grads)


def dot(a, b, dims):
    return lax.dot_general(a, b, (dims, ((), ())), precision=HIGHEST, preferred_element_type=jnp.float32)


def one_hots(idx_ref):
    places = lax.broadcasted_iota(jnp.int32, (SIDE, BAND), 0)
    masks = []
    for layer in range(LAYERS):
        idx = idx_ref[0, layer : layer + 1, :]
        rows = (idx // SIDE == places).astype(jnp.float32)
        cols = (idx % SIDE == places).astype(jnp.float32)
        masks.append(dot(rows, cols, ((1,), (1,))))
    return jnp.concatenate(masks, axis=1)


def encode_kernel(parts_ref, mom_ref, idx_ref, left_ref, wide_ref, new_ref, sent_ref):
    gradient = parts_ref[0]
    for k in range(1, parts_ref.shape[0]):
        gradient = gradient + parts_ref[k]
    pre = MOMENTUM_DECAY * mom_ref[0, 0] + gradient
    mask = one_hots(idx_ref)
    coeffs = dot(dot(left_ref[...], pre, ((1,), (0,))), wide_ref[...], ((1,), (1,)))
    kept = coeffs * mask
    for k in range(REPLICAS):
        sent_ref[k] = kept
    back = dot(dot(left_ref[...], kept, ((0,), (0,))), wide_ref[...], ((1,), (0,)))
    new_ref[0, 0] = pre - back


def decode_kernel(every_ref, left_ref, wide_ref, out_ref):
    mean = ((every_ref[0] + every_ref[1]) + (every_ref[2] + every_ref[3])) / REPLICAS
    back = dot(dot(left_ref[...], mean, ((0,), (0,))), wide_ref[...], ((1,), (0,)))
    out_ref[0] = DECODE_GAIN * back


def matrices():
    side = dct_matrix()
    return jnp.asarray(side), jnp.asarray(np.kron(np.eye(LAYERS, dtype=np.float32), side))


def encode(parts, momentum, band_idx):
    return pl.pallas_call(
        encode_kernel,
        out_shape=(
            jax.ShapeDtypeStruct((1, 1, SIDE, WIDE), jnp.float32),
            jax.ShapeDtypeStruct((REPLICAS, SIDE, WIDE), jnp.float32),
        ),
        compiler_params=pltpu.CompilerParams(vmem_limit_bytes=4 * 2**20),
        name="encode",
    )(parts, momentum, band_idx, *matrices())


def decode(every):
    return pl.pallas_call(
        decode_kernel,
        out_shape=jax.ShapeDtypeStruct((1, SIDE, WIDE), jnp.float32),
        compiler_params=pltpu.CompilerParams(vmem_limit_bytes=4 * 2**20),
        name="decode",
    )(every, *matrices())


def local(acts, grads, momentum, band_idx):
    second, third = stage_groups()
    axes = ("replica", "shard")
    exchange = functools.partial(lax.all_to_all, axis_name=axes, split_axis=0, concat_axis=0, tiled=True)
    place = lax.axis_index(axes)[None]
    acts = acts[0].transpose(1, 2, 0)
    hop = functools.partial(lax.ppermute, axis_name=axes)
    across_z, across_y = pairs(True, False), pairs(False, True)
    far0_other, far0_own, left = gradient_terms(place, acts, grads, 0, 1)
    far1_other, far1_own = gradient_terms(place, left, grads, 1, 1)
    near0_other, near0_own = gradient_terms(place, left, grads, 0, 0)
    near1_other, near1_own = gradient_terms(place, left, grads, 1, 0)
    far0 = far0_own + hop(far0_other, perm=across_y)
    other1 = near1_other + hop(far1_other, perm=across_z)
    sum0 = near0_own + hop(near0_other, perm=across_y) + hop(far0, perm=across_z)
    sum1 = near1_own + hop(far1_own, perm=across_z) + hop(other1, perm=across_y)
    terms = jnp.concatenate([sum0, sum1]).reshape(8, 6, SIDE, WIDE)
    terms = exchange(terms, axis_index_groups=second)
    terms = jnp.sum(terms, axis=0)
    terms = exchange(terms, axis_index_groups=third)
    new_momentum, sent = encode(terms, momentum, band_idx)
    every = lax.all_to_all(sent, "replica", split_axis=0, concat_axis=0, tiled=True)
    update = decode(every)
    return (new_momentum, update)


def solution(mesh):
    return jax.shard_map(
        local,
        mesh=mesh,
        in_specs=(
            P("replica", "shard", None, None),
            P("replica", "shard", None, None),
            P("replica", "shard", None, None),
            P("shard", None, None),
        ),
        out_specs=(P("replica", "shard", None, None), P("shard", None, None)),
        check_vma=False,
    )
```

```python
import functools

import jax
import jax.numpy as jnp
import numpy as np
from jax import lax
from jax.experimental import pallas as pl
from jax.experimental.pallas import tpu as pltpu
from jax.sharding import PartitionSpec as P

MOMENTUM_DECAY = 0.999
DECODE_GAIN = 8.0
SIDE = 64
LAYERS = 2
WIDE = SIDE * LAYERS
BAND = 32
REPLICAS = 4
CHUNK = 512
FIRST_VMEM = 50
HIGHEST = lax.Precision.HIGHEST


Z, Y = 12, 8


def flat(x_lo, core, z, x_hi, y):
    return ((x_lo * 2 + core) * Z + z % Z) * 16 + x_hi * 8 + y % Y


def partner(at, core, size):
    return (((at + size - core) ^ 1) + core) % size


def pairs(across_z, across_y, across_x=False):
    return [
        (
            flat(x_lo, core, z, x_hi, y),
            flat(
                x_lo,
                core,
                partner(z, core, Z) if across_z else z,
                1 - x_hi if across_x else x_hi,
                partner(y, core, Y) if across_y else y,
            ),
        )
        for x_lo in range(2)
        for core in range(2)
        for z in range(Z)
        for x_hi in range(2)
        for y in range(Y)
    ]


def stage_groups():
    return [
        [
            flat(x_lo, core, 4 * a + 2 * z1 + z0, x_hi, 4 * b + 2 * y1 + y0)
            for z1 in range(2)
            for y1 in range(2)
            for a in range(Z // 4)
            for b in range(Y // 4)
        ]
        for x_lo in range(2)
        for core in range(2)
        for x_hi in range(2)
        for z0 in range(2)
        for y0 in range(2)
    ]


def dct_matrix():
    u = np.arange(SIDE, dtype=np.float64)[:, None]
    x = np.arange(SIDE, dtype=np.float64)[None, :]
    scale = np.where(u == 0, np.sqrt(1.0 / SIDE), np.sqrt(2.0 / SIDE))
    return (scale * np.cos(np.pi * (2.0 * x + 1.0) * u / (2.0 * SIDE))).astype(np.float32)


def parities(place_ref):
    return (place_ref[0] >> 4) & 1, place_ref[0] & 1, (place_ref[0] >> 3) & 1


def left_kernel_part(act_ref, left_ref):
    rows, tokens = act_ref.shape[1:]
    token = lax.broadcasted_iota(jnp.int32, (tokens, tokens * LAYERS), 0)
    place = lax.broadcasted_iota(jnp.int32, (tokens, tokens * LAYERS), 1)
    for layer in range(LAYERS):
        spread = (place == token * LAYERS + layer).astype(jnp.float32).astype(act_ref.dtype)
        left_ref[layer * rows : (layer + 1) * rows] = jnp.dot(
            act_ref[layer], spread, preferred_element_type=jnp.float32
        ).astype(act_ref.dtype)


def terms_kernel(first, place_ref, in_ref, grad_ref, other_ref, own_ref, *made_ref):
    tokens = grad_ref.shape[1]
    if first:
        left_ref = made_ref[0]
        pl.when(pl.program_id(0) == 0)(lambda: left_kernel_part(in_ref, left_ref))
    else:
        left_ref = in_ref
    rows = left_ref.shape[0] // LAYERS
    rhs = grad_ref[0].reshape(tokens * LAYERS, CHUNK)
    both = jnp.dot(left_ref[...], rhs, preferred_element_type=jnp.float32)
    low = lax.broadcasted_iota(jnp.int32, (SIDE, WIDE), 1) < SIDE

    def write(even_ref, odd_ref):
        for a in range(rows // SIDE):
            for pair in range(CHUNK // WIDE):
                cols = slice(pair * WIDE, (pair + 1) * WIDE)
                one = both[a * SIDE : (a + 1) * SIDE, cols]
                two = both[rows + a * SIDE : rows + (a + 1) * SIDE, cols]
                even_ref[0, pair % 2, a, pair // 2] = jnp.where(low, one, pltpu.roll(two, SIDE, 1))
                odd_ref[0, pair % 2, a, pair // 2] = jnp.where(low, pltpu.roll(one, SIDE, 1), two)

    _, y_own, _ = parities(place_ref)
    pl.when(y_own == 0)(lambda: write(own_ref, other_ref))
    pl.when(y_own == 1)(lambda: write(other_ref, own_ref))


def gradient_terms(place, acts_or_left, grads, colour, far):
    first = acts_or_left.ndim == 3
    tokens = grads.shape[1]
    rows = acts_or_left.shape[1] if first else acts_or_left.shape[0] // LAYERS
    blocks = (2, 2, rows // SIDE, 2, SIDE, WIDE)
    out = jax.ShapeDtypeStruct(blocks, jnp.float32)
    out_spec = pl.BlockSpec((1,) + blocks[1:], lambda k, place: (k, 0, 0, 0, 0, 0))
    left = (LAYERS * rows, tokens * LAYERS)
    left_spec = pl.BlockSpec(left, lambda k, place: (0, 0))
    return pl.pallas_call(
        functools.partial(terms_kernel, first),
        grid_spec=pltpu.PrefetchScalarGridSpec(
            num_scalar_prefetch=1,
            grid=(2,),
            in_specs=[
                pl.BlockSpec(acts_or_left.shape, lambda k, place: (0, 0, 0)) if first else left_spec,
                pl.BlockSpec(
                    (1, tokens, LAYERS, CHUNK),
                    lambda k, place: (
                        0,
                        0,
                        0,
                        k * 4 + (parities(place)[0] ^ far) * 2 + (parities(place)[2] ^ colour),
                    ),
                ),
            ],
            out_specs=[out_spec, out_spec] + [left_spec] * first,
        ),
        out_shape=[out, out] + [jax.ShapeDtypeStruct(left, acts_or_left.dtype)] * first,
        compiler_params=pltpu.CompilerParams(vmem_limit_bytes=(FIRST_VMEM if first else 40) * 2**20),
        name=f"terms{colour}{far}",
    )(place, acts_or_left, grads)


def dot(a, b, dims):
    return lax.dot_general(a, b, (dims, ((), ())), precision=HIGHEST, preferred_element_type=jnp.float32)


def one_hots(idx_ref):
    places = lax.broadcasted_iota(jnp.int32, (SIDE, BAND), 0)
    masks = []
    for layer in range(LAYERS):
        idx = idx_ref[0, layer : layer + 1, :]
        rows = (idx // SIDE == places).astype(jnp.float32)
        cols = (idx % SIDE == places).astype(jnp.float32)
        masks.append(dot(rows, cols, ((1,), (1,))))
    return jnp.concatenate(masks, axis=1)


def encode_kernel(parts_ref, mom_ref, idx_ref, left_ref, wide_ref, new_ref, sent_ref):
    gradient = parts_ref[0]
    for k in range(1, parts_ref.shape[0]):
        gradient = gradient + parts_ref[k]
    pre = MOMENTUM_DECAY * mom_ref[0, 0] + gradient
    mask = one_hots(idx_ref)
    coeffs = dot(dot(left_ref[...], pre, ((1,), (0,))), wide_ref[...], ((1,), (1,)))
    kept = coeffs * mask
    for k in range(REPLICAS):
        sent_ref[k] = kept
    back = dot(dot(left_ref[...], kept, ((0,), (0,))), wide_ref[...], ((1,), (0,)))
    new_ref[0, 0] = pre - back


def decode_kernel(every_ref, left_ref, wide_ref, out_ref):
    mean = ((every_ref[0] + every_ref[1]) + (every_ref[2] + every_ref[3])) / REPLICAS
    back = dot(dot(left_ref[...], mean, ((0,), (0,))), wide_ref[...], ((1,), (0,)))
    out_ref[0] = DECODE_GAIN * back


def matrices():
    side = dct_matrix()
    return jnp.asarray(side), jnp.asarray(np.kron(np.eye(LAYERS, dtype=np.float32), side))


def encode(parts, momentum, band_idx):
    return pl.pallas_call(
        encode_kernel,
        out_shape=(
            jax.ShapeDtypeStruct((1, 1, SIDE, WIDE), jnp.float32),
            jax.ShapeDtypeStruct((REPLICAS, SIDE, WIDE), jnp.float32),
        ),
        compiler_params=pltpu.CompilerParams(vmem_limit_bytes=4 * 2**20),
        name="encode",
    )(parts, momentum, band_idx, *matrices())


def decode(every):
    return pl.pallas_call(
        decode_kernel,
        out_shape=jax.ShapeDtypeStruct((1, SIDE, WIDE), jnp.float32),
        compiler_params=pltpu.CompilerParams(vmem_limit_bytes=4 * 2**20),
        name="decode",
    )(every, *matrices())


def local(acts, grads, momentum, band_idx):
    axes = ("replica", "shard")
    exchange = functools.partial(lax.all_to_all, axis_name=axes, split_axis=0, concat_axis=0, tiled=True)
    place = lax.axis_index(axes)[None]
    acts = acts[0].transpose(1, 2, 0)
    hop = functools.partial(lax.ppermute, axis_name=axes)
    across_z, across_y, across_x = pairs(True, False), pairs(False, True), pairs(False, False, True)
    far0_other, far0_own, left = gradient_terms(place, acts, grads, 0, 1)
    far1_other, far1_own = gradient_terms(place, left, grads, 1, 1)
    near0_other, near0_own = gradient_terms(place, left, grads, 0, 0)
    near1_other, near1_own = gradient_terms(place, left, grads, 1, 0)
    far0 = far0_own + hop(far0_other, perm=across_y)
    other1 = near1_other + hop(far1_other, perm=across_z)
    sum0 = near0_own + hop(near0_other, perm=across_y) + hop(far0, perm=across_z)
    sum1 = near1_own + hop(far1_own, perm=across_z) + hop(other1, perm=across_y)
    terms = (sum0 + hop(sum1, perm=across_x)).reshape(24, SIDE, WIDE)
    terms = exchange(terms, axis_index_groups=stage_groups())
    new_momentum, sent = encode(terms, momentum, band_idx)
    every = lax.all_to_all(sent, "replica", split_axis=0, concat_axis=0, tiled=True)
    update = decode(every)
    return (new_momentum, update)


def solution(mesh):
    return jax.shard_map(
        local,
        mesh=mesh,
        in_specs=(
            P("replica", "shard", None, None),
            P("replica", "shard", None, None),
            P("replica", "shard", None, None),
            P("shard", None, None),
        ),
        out_specs=(P("replica", "shard", None, None), P("shard", None, None)),
        check_vma=False,
    )
```

```python
import functools

import jax
import jax.numpy as jnp
import numpy as np
from jax import lax
from jax.experimental import pallas as pl
from jax.experimental.pallas import tpu as pltpu
from jax.sharding import PartitionSpec as P

MOMENTUM_DECAY = 0.999
DECODE_GAIN = 8.0
SIDE = 64
LAYERS = 2
WIDE = SIDE * LAYERS
BAND = 32
REPLICAS = 4
CHUNK = 512
FIRST_VMEM = 50
HIGHEST = lax.Precision.HIGHEST


Z, Y = 12, 8


def flat(x_lo, core, z, x_hi, y):
    return ((x_lo * 2 + core) * Z + z % Z) * 16 + x_hi * 8 + y % Y


def partner(at, core, size):
    return (((at + size - core) ^ 1) + core) % size


def pairs(across_x, across_z, across_y, stride=1):
    def target(at, core, size, crossed):
        return stride * partner(at // stride, core, size // stride) + at % stride if crossed else at

    return [
        (
            flat(x_lo, core, z, x_hi, y),
            flat(x_lo, core, target(z, core, Z, across_z), x_hi ^ across_x, target(y, core, Y, across_y)),
        )
        for x_lo in range(2)
        for core in range(2)
        for z in range(Z)
        for x_hi in range(2)
        for y in range(Y)
    ]


def stage_groups():
    return [
        [flat(x_lo, core, 4 * a + z, x_hi, 4 * b + y) for a in range(Z // 4) for b in range(Y // 4)]
        for x_lo in range(2)
        for core in range(2)
        for x_hi in range(2)
        for z in range(4)
        for y in range(4)
    ]


def dct_matrix():
    u = np.arange(SIDE, dtype=np.float64)[:, None]
    x = np.arange(SIDE, dtype=np.float64)[None, :]
    scale = np.where(u == 0, np.sqrt(1.0 / SIDE), np.sqrt(2.0 / SIDE))
    return (scale * np.cos(np.pi * (2.0 * x + 1.0) * u / (2.0 * SIDE))).astype(np.float32)


def coordinates(place_ref):
    place = place_ref[0]
    core = lax.div(place, 192) & 1
    return core, lax.div(lax.rem(place, 192), 16), (place >> 3) & 1, place & 7


def left_kernel_part(act_ref, left_ref):
    rows, tokens = act_ref.shape[1:]
    token = lax.broadcasted_iota(jnp.int32, (tokens, tokens * LAYERS), 0)
    place = lax.broadcasted_iota(jnp.int32, (tokens, tokens * LAYERS), 1)
    for layer in range(LAYERS):
        spread = (place == token * LAYERS + layer).astype(jnp.float32).astype(act_ref.dtype)
        left_ref[layer * rows : (layer + 1) * rows] = jnp.dot(
            act_ref[layer], spread, preferred_element_type=jnp.float32
        ).astype(act_ref.dtype)


def terms_kernel(first, place_ref, in_ref, grad_ref, other_ref, own_ref, *made_ref):
    tokens = grad_ref.shape[1]
    if first:
        left_ref = made_ref[0]
        pl.when(pl.program_id(0) == 0)(lambda: left_kernel_part(in_ref, left_ref))
    else:
        left_ref = in_ref
    rows = left_ref.shape[0] // LAYERS
    rhs = grad_ref[0].reshape(tokens * LAYERS, CHUNK)
    both = jnp.dot(left_ref[...], rhs, preferred_element_type=jnp.float32)
    low = lax.broadcasted_iota(jnp.int32, (SIDE, WIDE), 1) < SIDE

    core, _, _, y = coordinates(place_ref)
    other_bit = 1 ^ ((partner(y, core, Y) >> 1) & 1)
    own_bit = 1 ^ ((y >> 1) & 1)

    def write(even_ref, odd_ref, even_bit, odd_bit):
        for a in range(rows // SIDE):
            for pair in range(CHUNK // WIDE):
                cols = slice(pair * WIDE, (pair + 1) * WIDE)
                one = both[a * SIDE : (a + 1) * SIDE, cols]
                two = both[rows + a * SIDE : rows + (a + 1) * SIDE, cols]
                even = jnp.where(low, one, pltpu.roll(two, SIDE, 1))
                odd = jnp.where(low, pltpu.roll(one, SIDE, 1), two)
                even_ref[0, even_bit ^ (pair % 2), a, pair // 2] = even
                odd_ref[0, odd_bit ^ (pair % 2), a, pair // 2] = odd

    pl.when(y & 1 == 0)(lambda: write(own_ref, other_ref, own_bit, other_bit))
    pl.when(y & 1 == 1)(lambda: write(other_ref, own_ref, other_bit, own_bit))


def gradient_terms(place, acts_or_left, grads, colour, far):
    first = acts_or_left.ndim == 3

    def column_block(k, place):
        core, z, x, _ = coordinates(place)
        holder = partner(z, core, Z) if far else z
        return (0, 0, 0, (k ^ 1 ^ ((holder >> 1) & 1)) * 4 + (holder & 1) * 2 + (x ^ colour))

    tokens = grads.shape[1]
    rows = acts_or_left.shape[1] if first else acts_or_left.shape[0] // LAYERS
    blocks = (2, 2, rows // SIDE, 2, SIDE, WIDE)
    out = jax.ShapeDtypeStruct(blocks, jnp.float32)
    out_spec = pl.BlockSpec((1,) + blocks[1:], lambda k, place: (k, 0, 0, 0, 0, 0))
    left = (LAYERS * rows, tokens * LAYERS)
    left_spec = pl.BlockSpec(left, lambda k, place: (0, 0))
    return pl.pallas_call(
        functools.partial(terms_kernel, first),
        grid_spec=pltpu.PrefetchScalarGridSpec(
            num_scalar_prefetch=1,
            grid=(2,),
            in_specs=[
                pl.BlockSpec(acts_or_left.shape, lambda k, place: (0, 0, 0)) if first else left_spec,
                pl.BlockSpec(
                    (1, tokens, LAYERS, CHUNK),
                    column_block,
                ),
            ],
            out_specs=[out_spec, out_spec] + [left_spec] * first,
        ),
        out_shape=[out, out] + [jax.ShapeDtypeStruct(left, acts_or_left.dtype)] * first,
        compiler_params=pltpu.CompilerParams(vmem_limit_bytes=(FIRST_VMEM if first else 40) * 2**20),
        name=f"terms{colour}{far}",
    )(place, acts_or_left, grads)


def dot(a, b, dims):
    return lax.dot_general(a, b, (dims, ((), ())), precision=HIGHEST, preferred_element_type=jnp.float32)


def one_hots(idx_ref):
    places = lax.broadcasted_iota(jnp.int32, (SIDE, BAND), 0)
    masks = []
    for layer in range(LAYERS):
        idx = idx_ref[0, layer : layer + 1, :]
        rows = (idx // SIDE == places).astype(jnp.float32)
        cols = (idx % SIDE == places).astype(jnp.float32)
        masks.append(dot(rows, cols, ((1,), (1,))))
    return jnp.concatenate(masks, axis=1)


def encode_kernel(parts_ref, mom_ref, idx_ref, left_ref, wide_ref, new_ref, sent_ref):
    gradient = parts_ref[0]
    for k in range(1, parts_ref.shape[0]):
        gradient = gradient + parts_ref[k]
    pre = MOMENTUM_DECAY * mom_ref[0, 0] + gradient
    mask = one_hots(idx_ref)
    coeffs = dot(dot(left_ref[...], pre, ((1,), (0,))), wide_ref[...], ((1,), (1,)))
    kept = coeffs * mask
    for k in range(REPLICAS):
        sent_ref[k] = kept
    back = dot(dot(left_ref[...], kept, ((0,), (0,))), wide_ref[...], ((1,), (0,)))
    new_ref[0, 0] = pre - back


def decode_kernel(every_ref, left_ref, wide_ref, out_ref):
    mean = ((every_ref[0] + every_ref[1]) + (every_ref[2] + every_ref[3])) / REPLICAS
    back = dot(dot(left_ref[...], mean, ((0,), (0,))), wide_ref[...], ((1,), (0,)))
    out_ref[0] = DECODE_GAIN * back


def matrices():
    side = dct_matrix()
    return jnp.asarray(side), jnp.asarray(np.kron(np.eye(LAYERS, dtype=np.float32), side))


def encode(parts, momentum, band_idx):
    return pl.pallas_call(
        encode_kernel,
        out_shape=(
            jax.ShapeDtypeStruct((1, 1, SIDE, WIDE), jnp.float32),
            jax.ShapeDtypeStruct((REPLICAS, SIDE, WIDE), jnp.float32),
        ),
        compiler_params=pltpu.CompilerParams(vmem_limit_bytes=4 * 2**20),
        name="encode",
    )(parts, momentum, band_idx, *matrices())


def decode(every):
    return pl.pallas_call(
        decode_kernel,
        out_shape=jax.ShapeDtypeStruct((1, SIDE, WIDE), jnp.float32),
        compiler_params=pltpu.CompilerParams(vmem_limit_bytes=4 * 2**20),
        name="decode",
    )(every, *matrices())


def local(acts, grads, momentum, band_idx):
    axes = ("replica", "shard")
    exchange = functools.partial(lax.all_to_all, axis_name=axes, split_axis=0, concat_axis=0, tiled=True)
    place = lax.axis_index(axes)[None]
    acts = acts[0].transpose(1, 2, 0)
    hop = functools.partial(lax.ppermute, axis_name=axes)
    across_z, across_y = pairs(0, 1, 0), pairs(0, 0, 1)
    far1_other, far1_own, left = gradient_terms(place, acts, grads, 1, 1)
    far0_other, far0_own = gradient_terms(place, left, grads, 0, 1)
    near0_other, near0_own = gradient_terms(place, left, grads, 0, 0)
    near1_other, near1_own = gradient_terms(place, left, grads, 1, 0)
    near0_other, near1_other = lax.optimization_barrier((near0_other, near1_other))
    far0 = far0_own + hop(far0_other, perm=across_y)
    other1 = near1_other + hop(far1_other, perm=across_z)
    sum0 = near0_own + hop(near0_other, perm=across_y) + hop(far0, perm=across_z)
    sum1 = near1_own + hop(far1_own, perm=across_z) + hop(other1, perm=across_y)
    terms = sum0[1, 1]
    for other_x, piece in ((1, sum1), (0, sum0)):
        for z_like, y_like in ((0, 0), (0, 1), (1, 0), (1, 1)):
            if other_x or not (z_like and y_like):
                terms += hop(piece[z_like, y_like], perm=pairs(other_x, 1 - z_like, 1 - y_like, 2))
    terms = exchange(terms.reshape(6, SIDE, WIDE), axis_index_groups=stage_groups())
    new_momentum, sent = encode(terms, momentum, band_idx)
    every = lax.all_to_all(sent, "replica", split_axis=0, concat_axis=0, tiled=True)
    update = decode(every)
    return (new_momentum, update)


def solution(mesh):
    return jax.shard_map(
        local,
        mesh=mesh,
        in_specs=(
            P("replica", "shard", None, None),
            P("replica", "shard", None, None),
            P("replica", "shard", None, None),
            P("shard", None, None),
        ),
        out_specs=(P("replica", "shard", None, None), P("shard", None, None)),
        check_vma=False,
    )
```

```python
import functools

import jax
import jax.numpy as jnp
import numpy as np
from jax import lax
from jax.experimental import pallas as pl
from jax.experimental.pallas import tpu as pltpu
from jax.sharding import PartitionSpec as P

MOMENTUM_DECAY = 0.999
DECODE_GAIN = 8.0
SIDE = 64
LAYERS = 2
WIDE = SIDE * LAYERS
BAND = 32
REPLICAS = 4
CHUNK = 512
FIRST_VMEM = 50
HIGHEST = lax.Precision.HIGHEST


Z, Y = 12, 8


def flat(x_lo, core, z, x_hi, y):
    return ((x_lo * 2 + core) * Z + z % Z) * 16 + x_hi * 8 + y % Y


def partner(at, core, size):
    return (((at + size - core) ^ 1) + core) % size


def pairs(across_z, across_y):
    return [
        (
            flat(x_lo, core, z, x_hi, y),
            flat(
                x_lo,
                core,
                partner(z, core, Z) if across_z else z,
                x_hi,
                partner(y, core, Y) if across_y else y,
            ),
        )
        for x_lo in range(2)
        for core in range(2)
        for z in range(Z)
        for x_hi in range(2)
        for y in range(Y)
    ]


def stage_groups():
    second, third = [], []
    for x_lo in range(2):
        for core in range(2):
            for z0 in range(2):
                for y0 in range(2):
                    for m in range(core, 6 + core, 2):
                        for n in range(core, 4 + core, 2):
                            pz = sorted((m % 6, (m + 1) % 6), key=lambda v: v % 2)
                            py = sorted((n % 4, (n + 1) % 4), key=lambda v: v % 2)
                            second.append(
                                [
                                    flat(x_lo, core, 2 * a + z0, h, 2 * b + y0)
                                    for h in range(2)
                                    for a in pz
                                    for b in py
                                ]
                            )
            for x_hi in range(2):
                for z in range(4):
                    for y in range(4):
                        third.append(
                            [flat(x_lo, core, 4 * a + z, x_hi, 4 * b + y) for a in range(3) for b in range(2)]
                        )
    return second, third


def dct_matrix():
    u = np.arange(SIDE, dtype=np.float64)[:, None]
    x = np.arange(SIDE, dtype=np.float64)[None, :]
    scale = np.where(u == 0, np.sqrt(1.0 / SIDE), np.sqrt(2.0 / SIDE))
    return (scale * np.cos(np.pi * (2.0 * x + 1.0) * u / (2.0 * SIDE))).astype(np.float32)


def parities(place_ref):
    return (place_ref[0] >> 4) & 1, place_ref[0] & 1


def left_kernel_part(act_ref, left_ref):
    rows, tokens = act_ref.shape[1:]
    token = lax.broadcasted_iota(jnp.int32, (tokens, tokens * LAYERS), 0)
    place = lax.broadcasted_iota(jnp.int32, (tokens, tokens * LAYERS), 1)
    for layer in range(LAYERS):
        spread = (place == token * LAYERS + layer).astype(jnp.float32).astype(act_ref.dtype)
        left_ref[layer * rows : (layer + 1) * rows] = jnp.dot(
            act_ref[layer], spread, preferred_element_type=jnp.float32
        ).astype(act_ref.dtype)


def terms_kernel(first, place_ref, in_ref, grad_ref, other_ref, own_ref, *made_ref):
    tokens = grad_ref.shape[1]
    if first:
        left_ref = made_ref[0]
        pl.when(pl.program_id(0) == 0)(lambda: left_kernel_part(in_ref, left_ref))
    else:
        left_ref = in_ref
    rows = left_ref.shape[0] // LAYERS
    rhs = grad_ref[0].reshape(tokens * LAYERS, CHUNK)
    both = jnp.dot(left_ref[...], rhs, preferred_element_type=jnp.float32)
    low = lax.broadcasted_iota(jnp.int32, (SIDE, WIDE), 1) < SIDE

    def write(even_ref, odd_ref):
        for a in range(rows // SIDE):
            for pair in range(CHUNK // WIDE):
                cols = slice(pair * WIDE, (pair + 1) * WIDE)
                one = both[a * SIDE : (a + 1) * SIDE, cols]
                two = both[rows + a * SIDE : rows + (a + 1) * SIDE, cols]
                even_ref[0, pair % 2, a, pair // 2] = jnp.where(low, one, pltpu.roll(two, SIDE, 1))
                odd_ref[0, pair % 2, a, pair // 2] = jnp.where(low, pltpu.roll(one, SIDE, 1), two)

    _, y_own = parities(place_ref)
    pl.when(y_own == 0)(lambda: write(own_ref, other_ref))
    pl.when(y_own == 1)(lambda: write(other_ref, own_ref))


def gradient_terms(place, acts_or_left, grads, colour, far):
    first = acts_or_left.ndim == 3
    tokens = grads.shape[1]
    rows = acts_or_left.shape[1] if first else acts_or_left.shape[0] // LAYERS
    blocks = (2, 2, rows // SIDE, 2, SIDE, WIDE)
    out = jax.ShapeDtypeStruct(blocks, jnp.float32)
    out_spec = pl.BlockSpec((1,) + blocks[1:], lambda k, place: (k, 0, 0, 0, 0, 0))
    left = (LAYERS * rows, tokens * LAYERS)
    left_spec = pl.BlockSpec(left, lambda k, place: (0, 0))
    return pl.pallas_call(
        functools.partial(terms_kernel, first),
        grid_spec=pltpu.PrefetchScalarGridSpec(
            num_scalar_prefetch=1,
            grid=(2,),
            in_specs=[
                pl.BlockSpec(acts_or_left.shape, lambda k, place: (0, 0, 0)) if first else left_spec,
                pl.BlockSpec(
                    (1, tokens, LAYERS, CHUNK),
                    lambda k, place: (0, 0, 0, k * 4 + (parities(place)[0] ^ far) * 2 + colour),
                ),
            ],
            out_specs=[out_spec, out_spec] + [left_spec] * first,
        ),
        out_shape=[out, out] + [jax.ShapeDtypeStruct(left, acts_or_left.dtype)] * first,
        compiler_params=pltpu.CompilerParams(vmem_limit_bytes=(FIRST_VMEM if first else 40) * 2**20),
        name=f"terms{colour}{far}",
    )(place, acts_or_left, grads)


def dot(a, b, dims):
    return lax.dot_general(a, b, (dims, ((), ())), precision=HIGHEST, preferred_element_type=jnp.float32)


def one_hots(idx_ref):
    places = lax.broadcasted_iota(jnp.int32, (SIDE, BAND), 0)
    masks = []
    for layer in range(LAYERS):
        idx = idx_ref[0, layer : layer + 1, :]
        rows = (idx // SIDE == places).astype(jnp.float32)
        cols = (idx % SIDE == places).astype(jnp.float32)
        masks.append(dot(rows, cols, ((1,), (1,))))
    return jnp.concatenate(masks, axis=1)


def encode_kernel(parts_ref, mom_ref, idx_ref, left_ref, wide_ref, new_ref, sent_ref):
    gradient = parts_ref[0]
    for k in range(1, parts_ref.shape[0]):
        gradient = gradient + parts_ref[k]
    pre = MOMENTUM_DECAY * mom_ref[0, 0] + gradient
    mask = one_hots(idx_ref)
    coeffs = dot(dot(left_ref[...], pre, ((1,), (0,))), wide_ref[...], ((1,), (1,)))
    kept = coeffs * mask
    for k in range(REPLICAS):
        sent_ref[k] = kept
    back = dot(dot(left_ref[...], kept, ((0,), (0,))), wide_ref[...], ((1,), (0,)))
    new_ref[0, 0] = pre - back


def decode_kernel(every_ref, left_ref, wide_ref, out_ref):
    mean = ((every_ref[0] + every_ref[1]) + (every_ref[2] + every_ref[3])) / REPLICAS
    back = dot(dot(left_ref[...], mean, ((0,), (0,))), wide_ref[...], ((1,), (0,)))
    out_ref[0] = DECODE_GAIN * back


def matrices():
    side = dct_matrix()
    return jnp.asarray(side), jnp.asarray(np.kron(np.eye(LAYERS, dtype=np.float32), side))


def encode(parts, momentum, band_idx):
    return pl.pallas_call(
        encode_kernel,
        out_shape=(
            jax.ShapeDtypeStruct((1, 1, SIDE, WIDE), jnp.float32),
            jax.ShapeDtypeStruct((REPLICAS, SIDE, WIDE), jnp.float32),
        ),
        compiler_params=pltpu.CompilerParams(vmem_limit_bytes=4 * 2**20),
        name="encode",
    )(parts, momentum, band_idx, *matrices())


def decode(every):
    return pl.pallas_call(
        decode_kernel,
        out_shape=jax.ShapeDtypeStruct((1, SIDE, WIDE), jnp.float32),
        compiler_params=pltpu.CompilerParams(vmem_limit_bytes=4 * 2**20),
        name="decode",
    )(every, *matrices())


def local(acts, grads, momentum, band_idx):
    second, third = stage_groups()
    axes = ("replica", "shard")
    exchange = functools.partial(lax.all_to_all, axis_name=axes, split_axis=0, concat_axis=0, tiled=True)
    place = lax.axis_index(axes)[None]
    acts = acts[0].transpose(1, 2, 0)
    hop = functools.partial(lax.ppermute, axis_name=axes)
    across_z, across_y = pairs(True, False), pairs(False, True)
    far1_other, far1_own, left = gradient_terms(place, acts, grads, 1, 1)
    far0_other, far0_own = gradient_terms(place, left, grads, 0, 1)
    near0_other, near0_own = gradient_terms(place, left, grads, 0, 0)
    near1_other, near1_own = gradient_terms(place, left, grads, 1, 0)
    near0_other, near1_other = lax.optimization_barrier((near0_other, near1_other))
    far0 = far0_own + hop(far0_other, perm=across_y)
    other1 = near1_other + hop(far1_other, perm=across_z)
    sum0 = near0_own + hop(near0_other, perm=across_y) + hop(far0, perm=across_z)
    sum1 = near1_own + hop(far1_own, perm=across_z) + hop(other1, perm=across_y)
    terms = jnp.concatenate([sum0, sum1]).reshape(8, 6, SIDE, WIDE)
    terms = exchange(terms, axis_index_groups=second)
    terms = jnp.sum(terms, axis=0)
    terms = exchange(terms, axis_index_groups=third)
    new_momentum, sent = encode(terms, momentum, band_idx)
    every = lax.all_to_all(sent, "replica", split_axis=0, concat_axis=0, tiled=True)
    update = decode(every)
    return (new_momentum, update)


def solution(mesh):
    return jax.shard_map(
        local,
        mesh=mesh,
        in_specs=(
            P("replica", "shard", None, None),
            P("replica", "shard", None, None),
            P("replica", "shard", None, None),
            P("shard", None, None),
        ),
        out_specs=(P("replica", "shard", None, None), P("shard", None, None)),
        check_vma=False,
    )
```

```python
import functools

import jax
import jax.numpy as jnp
import numpy as np
from jax import lax
from jax.experimental import pallas as pl
from jax.experimental.pallas import tpu as pltpu
from jax.sharding import PartitionSpec as P

MOMENTUM_DECAY = 0.999
DECODE_GAIN = 8.0
SIDE = 64
LAYERS = 2
WIDE = SIDE * LAYERS
BAND = 32
REPLICAS = 4
CHUNK = 512
FIRST_VMEM = 50
HIGHEST = lax.Precision.HIGHEST


Z, Y = 12, 8


def flat(x_lo, core, z, x_hi, y):
    return ((x_lo * 2 + core) * Z + z % Z) * 16 + x_hi * 8 + y % Y


def partner(at, core, size):
    return (((at + size - core) ^ 1) + core) % size


def pairs(across_x, across_z, across_y, stride=1):
    def target(at, core, size, crossed):
        return stride * partner(at // stride, core, size // stride) + at % stride if crossed else at

    return [
        (
            flat(x_lo, core, z, x_hi, y),
            flat(x_lo, core, target(z, core, Z, across_z), x_hi ^ across_x, target(y, core, Y, across_y)),
        )
        for x_lo in range(2)
        for core in range(2)
        for z in range(Z)
        for x_hi in range(2)
        for y in range(Y)
    ]


def stage_groups():
    return [
        [flat(x_lo, core, 4 * a + z, x_hi, 4 * b + y) for a in range(Z // 4) for b in range(Y // 4)]
        for x_lo in range(2)
        for core in range(2)
        for x_hi in range(2)
        for z in range(4)
        for y in range(4)
    ]


def dct_matrix():
    u = np.arange(SIDE, dtype=np.float64)[:, None]
    x = np.arange(SIDE, dtype=np.float64)[None, :]
    scale = np.where(u == 0, np.sqrt(1.0 / SIDE), np.sqrt(2.0 / SIDE))
    return (scale * np.cos(np.pi * (2.0 * x + 1.0) * u / (2.0 * SIDE))).astype(np.float32)


def coordinates(place_ref):
    place = place_ref[0]
    core = lax.div(place, 192) & 1
    return core, lax.div(lax.rem(place, 192), 16), (place >> 3) & 1, place & 7


def left_kernel_part(act_ref, left_ref):
    rows, tokens = act_ref.shape[1:]
    token = lax.broadcasted_iota(jnp.int32, (tokens, tokens * LAYERS), 0)
    place = lax.broadcasted_iota(jnp.int32, (tokens, tokens * LAYERS), 1)
    for layer in range(LAYERS):
        spread = (place == token * LAYERS + layer).astype(jnp.float32).astype(act_ref.dtype)
        left_ref[layer * rows : (layer + 1) * rows] = jnp.dot(
            act_ref[layer], spread, preferred_element_type=jnp.float32
        ).astype(act_ref.dtype)


def terms_kernel(first, place_ref, in_ref, grad_ref, other_ref, own_ref, *made_ref):
    tokens = grad_ref.shape[1]
    if first:
        left_ref = made_ref[0]
        pl.when(pl.program_id(0) == 0)(lambda: left_kernel_part(in_ref, left_ref))
    else:
        left_ref = in_ref
    rows = left_ref.shape[0] // LAYERS
    rhs = grad_ref[0].reshape(tokens * LAYERS, CHUNK)
    both = jnp.dot(left_ref[...], rhs, preferred_element_type=jnp.float32)
    low = lax.broadcasted_iota(jnp.int32, (SIDE, WIDE), 1) < SIDE

    core, _, _, y = coordinates(place_ref)
    other_bit = 1 ^ ((partner(y, core, Y) >> 1) & 1)
    own_bit = 1 ^ ((y >> 1) & 1)

    def write(even_ref, odd_ref, even_bit, odd_bit):
        for a in range(rows // SIDE):
            for pair in range(CHUNK // WIDE):
                cols = slice(pair * WIDE, (pair + 1) * WIDE)
                one = both[a * SIDE : (a + 1) * SIDE, cols]
                two = both[rows + a * SIDE : rows + (a + 1) * SIDE, cols]
                even = jnp.where(low, one, pltpu.roll(two, SIDE, 1))
                odd = jnp.where(low, pltpu.roll(one, SIDE, 1), two)
                even_ref[0, even_bit ^ (pair % 2), a, pair // 2] = even
                odd_ref[0, odd_bit ^ (pair % 2), a, pair // 2] = odd

    pl.when(y & 1 == 0)(lambda: write(own_ref, other_ref, own_bit, other_bit))
    pl.when(y & 1 == 1)(lambda: write(other_ref, own_ref, other_bit, own_bit))


def gradient_terms(place, acts_or_left, grads, colour, far):
    first = acts_or_left.ndim == 3

    def column_block(k, place):
        core, z, x, _ = coordinates(place)
        holder = partner(z, core, Z) if far else z
        return (0, 0, 0, (k ^ 1 ^ ((holder >> 1) & 1)) * 4 + (holder & 1) * 2 + (x ^ colour))

    tokens = grads.shape[1]
    rows = acts_or_left.shape[1] if first else acts_or_left.shape[0] // LAYERS
    blocks = (2, 2, rows // SIDE, 2, SIDE, WIDE)
    out = jax.ShapeDtypeStruct(blocks, jnp.float32)
    out_spec = pl.BlockSpec((1,) + blocks[1:], lambda k, place: (k, 0, 0, 0, 0, 0))
    left = (LAYERS * rows, tokens * LAYERS)
    left_spec = pl.BlockSpec(left, lambda k, place: (0, 0))
    return pl.pallas_call(
        functools.partial(terms_kernel, first),
        grid_spec=pltpu.PrefetchScalarGridSpec(
            num_scalar_prefetch=1,
            grid=(2,),
            in_specs=[
                pl.BlockSpec(acts_or_left.shape, lambda k, place: (0, 0, 0)) if first else left_spec,
                pl.BlockSpec(
                    (1, tokens, LAYERS, CHUNK),
                    column_block,
                ),
            ],
            out_specs=[out_spec, out_spec] + [left_spec] * first,
        ),
        out_shape=[out, out] + [jax.ShapeDtypeStruct(left, acts_or_left.dtype)] * first,
        compiler_params=pltpu.CompilerParams(vmem_limit_bytes=(FIRST_VMEM if first else 40) * 2**20),
        name=f"terms{colour}{far}",
    )(place, acts_or_left, grads)


def dot(a, b, dims):
    return lax.dot_general(a, b, (dims, ((), ())), precision=HIGHEST, preferred_element_type=jnp.float32)


def one_hots(idx_ref):
    places = lax.broadcasted_iota(jnp.int32, (SIDE, BAND), 0)
    masks = []
    for layer in range(LAYERS):
        idx = idx_ref[0, layer : layer + 1, :]
        rows = (idx // SIDE == places).astype(jnp.float32)
        cols = (idx % SIDE == places).astype(jnp.float32)
        masks.append(dot(rows, cols, ((1,), (1,))))
    return jnp.concatenate(masks, axis=1)


def encode_kernel(parts_ref, mom_ref, idx_ref, left_ref, wide_ref, new_ref, sent_ref):
    gradient = parts_ref[0]
    for k in range(1, parts_ref.shape[0]):
        gradient = gradient + parts_ref[k]
    pre = MOMENTUM_DECAY * mom_ref[0, 0] + gradient
    mask = one_hots(idx_ref)
    coeffs = dot(dot(left_ref[...], pre, ((1,), (0,))), wide_ref[...], ((1,), (1,)))
    kept = coeffs * mask
    for k in range(REPLICAS):
        sent_ref[k] = kept
    back = dot(dot(left_ref[...], kept, ((0,), (0,))), wide_ref[...], ((1,), (0,)))
    new_ref[0, 0] = pre - back


def decode_kernel(every_ref, left_ref, wide_ref, out_ref):
    mean = ((every_ref[0] + every_ref[1]) + (every_ref[2] + every_ref[3])) / REPLICAS
    back = dot(dot(left_ref[...], mean, ((0,), (0,))), wide_ref[...], ((1,), (0,)))
    out_ref[0] = DECODE_GAIN * back


def matrices():
    side = dct_matrix()
    return jnp.asarray(side), jnp.asarray(np.kron(np.eye(LAYERS, dtype=np.float32), side))


def encode(parts, momentum, band_idx):
    return pl.pallas_call(
        encode_kernel,
        out_shape=(
            jax.ShapeDtypeStruct((1, 1, SIDE, WIDE), jnp.float32),
            jax.ShapeDtypeStruct((REPLICAS, SIDE, WIDE), jnp.float32),
        ),
        compiler_params=pltpu.CompilerParams(vmem_limit_bytes=4 * 2**20),
        name="encode",
    )(parts, momentum, band_idx, *matrices())


def decode(every):
    return pl.pallas_call(
        decode_kernel,
        out_shape=jax.ShapeDtypeStruct((1, SIDE, WIDE), jnp.float32),
        compiler_params=pltpu.CompilerParams(vmem_limit_bytes=4 * 2**20),
        name="decode",
    )(every, *matrices())


def local(acts, grads, momentum, band_idx):
    axes = ("replica", "shard")
    exchange = functools.partial(lax.all_to_all, axis_name=axes, split_axis=0, concat_axis=0, tiled=True)
    place = lax.axis_index(axes)[None]
    acts = acts[0].transpose(1, 2, 0)
    hop = functools.partial(lax.ppermute, axis_name=axes)
    across_z, across_y = pairs(0, 1, 0), pairs(0, 0, 1)
    far1_other, far1_own, left = gradient_terms(place, acts, grads, 1, 1)
    far0_other, far0_own = gradient_terms(place, left, grads, 0, 1)
    near0_other, near0_own = gradient_terms(place, left, grads, 0, 0)
    near1_other, near1_own = gradient_terms(place, left, grads, 1, 0)
    far0 = far0_own + hop(far0_other, perm=across_y)
    near0_other, far0 = lax.optimization_barrier((near0_other, far0))
    other1 = near1_other + hop(far1_other, perm=across_z)
    sum0 = near0_own + hop(near0_other, perm=across_y) + hop(far0, perm=across_z)
    sum1 = near1_own + hop(far1_own, perm=across_z) + hop(other1, perm=across_y)
    terms = sum0[1, 1]
    for other_x, piece in ((1, sum1), (0, sum0)):
        for z_like, y_like in ((0, 0), (0, 1), (1, 0), (1, 1)):
            if other_x or not (z_like and y_like):
                terms += hop(piece[z_like, y_like], perm=pairs(other_x, 1 - z_like, 1 - y_like, 2))
    terms = exchange(terms.reshape(6, SIDE, WIDE), axis_index_groups=stage_groups())
    new_momentum, sent = encode(terms, momentum, band_idx)
    every = lax.all_to_all(sent, "replica", split_axis=0, concat_axis=0, tiled=True)
    update = decode(every)
    return (new_momentum, update)


def solution(mesh):
    return jax.shard_map(
        local,
        mesh=mesh,
        in_specs=(
            P("replica", "shard", None, None),
            P("replica", "shard", None, None),
            P("replica", "shard", None, None),
            P("shard", None, None),
        ),
        out_specs=(P("replica", "shard", None, None), P("shard", None, None)),
        check_vma=False,
    )
```

```python
import functools

import jax
import jax.numpy as jnp
import numpy as np
from jax import lax
from jax.experimental import pallas as pl
from jax.experimental.pallas import tpu as pltpu
from jax.sharding import PartitionSpec as P

MOMENTUM_DECAY = 0.999
DECODE_GAIN = 8.0
SIDE = 64
LAYERS = 2
WIDE = SIDE * LAYERS
BAND = 32
REPLICAS = 4
CHUNK = 512
FIRST_VMEM = 50
HIGHEST = lax.Precision.HIGHEST


Z, Y = 12, 8


def flat(x_lo, core, z, x_hi, y):
    return ((x_lo * 2 + core) * Z + z % Z) * 16 + x_hi * 8 + y % Y


def partner(at, core, size):
    return (((at + size - core) ^ 1) + core) % size


def pairs(across_x, across_z, across_y, stride=1):
    def target(at, core, size, crossed):
        return stride * partner(at // stride, core, size // stride) + at % stride if crossed else at

    return [
        (
            flat(x_lo, core, z, x_hi, y),
            flat(x_lo, core, target(z, core, Z, across_z), x_hi ^ across_x, target(y, core, Y, across_y)),
        )
        for x_lo in range(2)
        for core in range(2)
        for z in range(Z)
        for x_hi in range(2)
        for y in range(Y)
    ]


def stage_groups():
    return [
        [flat(x_lo, core, 4 * a + z, x_hi, 4 * b + y) for a in range(Z // 4) for b in range(Y // 4)]
        for x_lo in range(2)
        for core in range(2)
        for x_hi in range(2)
        for z in range(4)
        for y in range(4)
    ]


def dct_matrix():
    u = np.arange(SIDE, dtype=np.float64)[:, None]
    x = np.arange(SIDE, dtype=np.float64)[None, :]
    scale = np.where(u == 0, np.sqrt(1.0 / SIDE), np.sqrt(2.0 / SIDE))
    return (scale * np.cos(np.pi * (2.0 * x + 1.0) * u / (2.0 * SIDE))).astype(np.float32)


def coordinates(place_ref):
    place = place_ref[0]
    core = lax.div(place, 192) & 1
    return core, lax.div(lax.rem(place, 192), 16), (place >> 3) & 1, place & 7


def left_kernel_part(act_ref, left_ref):
    rows, tokens = act_ref.shape[1:]
    token = lax.broadcasted_iota(jnp.int32, (tokens, tokens * LAYERS), 0)
    place = lax.broadcasted_iota(jnp.int32, (tokens, tokens * LAYERS), 1)
    for layer in range(LAYERS):
        spread = (place == token * LAYERS + layer).astype(jnp.float32).astype(act_ref.dtype)
        left_ref[layer * rows : (layer + 1) * rows] = jnp.dot(
            act_ref[layer], spread, preferred_element_type=jnp.float32
        ).astype(act_ref.dtype)


def terms_kernel(first, place_ref, in_ref, grad_ref, other_ref, own_ref, *made_ref):
    tokens = grad_ref.shape[1]
    if first:
        left_ref = made_ref[0]
        pl.when(pl.program_id(0) == 0)(lambda: left_kernel_part(in_ref, left_ref))
    else:
        left_ref = in_ref
    rows = left_ref.shape[0] // LAYERS
    rhs = grad_ref[0].reshape(tokens * LAYERS, CHUNK)
    both = jnp.dot(left_ref[...], rhs, preferred_element_type=jnp.float32)
    low = lax.broadcasted_iota(jnp.int32, (SIDE, WIDE), 1) < SIDE

    core, _, _, y = coordinates(place_ref)
    other_bit = 1 ^ ((partner(y, core, Y) >> 1) & 1)
    own_bit = 1 ^ ((y >> 1) & 1)

    def write(even_ref, odd_ref, even_bit, odd_bit):
        for a in range(rows // SIDE):
            for pair in range(CHUNK // WIDE):
                cols = slice(pair * WIDE, (pair + 1) * WIDE)
                one = both[a * SIDE : (a + 1) * SIDE, cols]
                two = both[rows + a * SIDE : rows + (a + 1) * SIDE, cols]
                even = jnp.where(low, one, pltpu.roll(two, SIDE, 1))
                odd = jnp.where(low, pltpu.roll(one, SIDE, 1), two)
                even_ref[0, even_bit ^ (pair % 2), a, pair // 2] = even
                odd_ref[0, odd_bit ^ (pair % 2), a, pair // 2] = odd

    pl.when(y & 1 == 0)(lambda: write(own_ref, other_ref, own_bit, other_bit))
    pl.when(y & 1 == 1)(lambda: write(other_ref, own_ref, other_bit, own_bit))


def gradient_terms(place, acts_or_left, grads, colour, far):
    first = acts_or_left.ndim == 3

    def column_block(k, place):
        core, z, x, _ = coordinates(place)
        holder = partner(z, core, Z) if far else z
        return (0, 0, 0, (k ^ 1 ^ ((holder >> 1) & 1)) * 4 + (holder & 1) * 2 + (x ^ colour))

    tokens = grads.shape[1]
    rows = acts_or_left.shape[1] if first else acts_or_left.shape[0] // LAYERS
    blocks = (2, 2, rows // SIDE, 2, SIDE, WIDE)
    out = jax.ShapeDtypeStruct(blocks, jnp.float32)
    out_spec = pl.BlockSpec((1,) + blocks[1:], lambda k, place: (k, 0, 0, 0, 0, 0))
    left = (LAYERS * rows, tokens * LAYERS)
    left_spec = pl.BlockSpec(left, lambda k, place: (0, 0))
    return pl.pallas_call(
        functools.partial(terms_kernel, first),
        grid_spec=pltpu.PrefetchScalarGridSpec(
            num_scalar_prefetch=1,
            grid=(2,),
            in_specs=[
                pl.BlockSpec(acts_or_left.shape, lambda k, place: (0, 0, 0)) if first else left_spec,
                pl.BlockSpec(
                    (1, tokens, LAYERS, CHUNK),
                    column_block,
                ),
            ],
            out_specs=[out_spec, out_spec] + [left_spec] * first,
        ),
        out_shape=[out, out] + [jax.ShapeDtypeStruct(left, acts_or_left.dtype)] * first,
        compiler_params=pltpu.CompilerParams(vmem_limit_bytes=(FIRST_VMEM if first else 40) * 2**20),
        name=f"terms{colour}{far}",
    )(place, acts_or_left, grads)


def dot(a, b, dims):
    return lax.dot_general(a, b, (dims, ((), ())), precision=HIGHEST, preferred_element_type=jnp.float32)


def one_hots(idx_ref):
    places = lax.broadcasted_iota(jnp.int32, (SIDE, BAND), 0)
    masks = []
    for layer in range(LAYERS):
        idx = idx_ref[0, layer : layer + 1, :]
        rows = (idx // SIDE == places).astype(jnp.float32)
        cols = (idx % SIDE == places).astype(jnp.float32)
        masks.append(dot(rows, cols, ((1,), (1,))))
    return jnp.concatenate(masks, axis=1)


def mask_kernel(idx_ref, mask_ref):
    mask_ref[...] = one_hots(idx_ref)


def encode_kernel(parts_ref, mom_ref, mask_ref, left_ref, wide_ref, pre_ref, sent_ref):
    gradient = parts_ref[0]
    for k in range(1, parts_ref.shape[0]):
        gradient = gradient + parts_ref[k]
    pre = MOMENTUM_DECAY * mom_ref[0, 0] + gradient
    coeffs = dot(dot(left_ref[...], pre, ((1,), (0,))), wide_ref[...], ((1,), (1,)))
    kept = coeffs * mask_ref[...]
    pre_ref[...] = pre
    for k in range(REPLICAS):
        sent_ref[k] = kept


def residual_kernel(pre_ref, sent_ref, left_ref, wide_ref, new_ref):
    back = dot(dot(left_ref[...], sent_ref[0], ((0,), (0,))), wide_ref[...], ((1,), (0,)))
    new_ref[0, 0] = pre_ref[...] - back


def decode_kernel(every_ref, left_ref, wide_ref, out_ref):
    mean = ((every_ref[0] + every_ref[1]) + (every_ref[2] + every_ref[3])) / REPLICAS
    back = dot(dot(left_ref[...], mean, ((0,), (0,))), wide_ref[...], ((1,), (0,)))
    out_ref[0] = DECODE_GAIN * back


def matrices():
    side = dct_matrix()
    return jnp.asarray(side), jnp.asarray(np.kron(np.eye(LAYERS, dtype=np.float32), side))


def small_call(kernel, shape, name):
    return pl.pallas_call(
        kernel,
        out_shape=shape,
        compiler_params=pltpu.CompilerParams(vmem_limit_bytes=4 * 2**20),
        name=name,
    )


def encode(parts, momentum, band_idx):
    tile = jax.ShapeDtypeStruct((SIDE, WIDE), jnp.float32)
    every = jax.ShapeDtypeStruct((REPLICAS, SIDE, WIDE), jnp.float32)
    mask = small_call(mask_kernel, tile, "mask")(band_idx)
    return small_call(encode_kernel, (tile, every), "encode")(parts, momentum, mask, *matrices())


def residual(pre, sent):
    shape = jax.ShapeDtypeStruct((1, 1, SIDE, WIDE), jnp.float32)
    return small_call(residual_kernel, shape, "residual")(pre, sent, *matrices())


def decode(every):
    return pl.pallas_call(
        decode_kernel,
        out_shape=jax.ShapeDtypeStruct((1, SIDE, WIDE), jnp.float32),
        compiler_params=pltpu.CompilerParams(vmem_limit_bytes=4 * 2**20),
        name="decode",
    )(every, *matrices())


def local(acts, grads, momentum, band_idx):
    axes = ("replica", "shard")
    exchange = functools.partial(lax.all_to_all, axis_name=axes, split_axis=0, concat_axis=0, tiled=True)
    place = lax.axis_index(axes)[None]
    acts = acts[0].transpose(1, 2, 0)
    hop = functools.partial(lax.ppermute, axis_name=axes)
    across_z, across_y = pairs(0, 1, 0), pairs(0, 0, 1)
    far1_other, far1_own, left = gradient_terms(place, acts, grads, 1, 1)
    far0_other, far0_own = gradient_terms(place, left, grads, 0, 1)
    near0_other, near0_own = gradient_terms(place, left, grads, 0, 0)
    near1_other, near1_own = gradient_terms(place, left, grads, 1, 0)
    far0 = far0_own + hop(far0_other, perm=across_y)
    near0_other, far0 = lax.optimization_barrier((near0_other, far0))
    other1 = near1_other + hop(far1_other, perm=across_z)
    sum0 = near0_own + hop(near0_other, perm=across_y) + hop(far0, perm=across_z)
    sum1 = near1_own + hop(far1_own, perm=across_z) + hop(other1, perm=across_y)
    terms = sum0[1, 1]
    for other_x, piece in ((1, sum1), (0, sum0)):
        for z_like, y_like in ((0, 0), (0, 1), (1, 0), (1, 1)):
            if other_x or not (z_like and y_like):
                terms += hop(piece[z_like, y_like], perm=pairs(other_x, 1 - z_like, 1 - y_like, 2))
    terms = exchange(terms.reshape(6, SIDE, WIDE), axis_index_groups=stage_groups())
    pre, sent = encode(terms, momentum, band_idx)
    every = lax.all_to_all(sent, "replica", split_axis=0, concat_axis=0, tiled=True)
    new_momentum = residual(pre, sent)
    update = decode(every)
    return (new_momentum, update)


def solution(mesh):
    return jax.shard_map(
        local,
        mesh=mesh,
        in_specs=(
            P("replica", "shard", None, None),
            P("replica", "shard", None, None),
            P("replica", "shard", None, None),
            P("shard", None, None),
        ),
        out_specs=(P("replica", "shard", None, None), P("shard", None, None)),
        check_vma=False,
    )
```
